256 devices in a mesh: ctx: 64 (over z, x, core), ch: 4 (over y).
Axes of the slice: x: 4, y: 4, z: 8, core: 2. Of those that a mesh axis runs over, the one named last changes fastest.
Arguments:
- streams: bfloat16 [3, 16384, 4096], P(None, 'ctx', 'ch'), may hold values from -6 to 6
- residual_in: bfloat16 [16384, 4096], P('ctx', 'ch'), may hold values from -6 to 6
- short_filter: float32 [3, 7, 4096], replicated, may hold values from -2 to 2
- medium_filter: bfloat16 [128, 4096], P(None, 'ch'), may hold values from -4 to 4
- skip_gain: float32 [4096], P('ch'), may hold values from -4 to 4
- w_out: bfloat16 [4096, 4096], P(('ch', 'ctx')), may hold values from -0.375 to 0.375
Outputs:
- block_out: bfloat16 [16384, 4096], P('ctx', 'ch')
The draws below stay inside these ranges and needn't reach their ends.
All inputs are finite; a program needn't handle non-finite values.
Results may differ from the reference program's by a relative error of at most 0.019.
Values may be sent and summed in bfloat16 or wider, within the bound.
A program may use at most 256 MiB of HBM per device.

```python
import math
import jax
import jax.numpy as jnp
from jax import lax

D = 4096
FILT = 128
SHORT = 7
TOK_DEV = 256
TOKENS = 16384
N_CTX = 64
N_CH = 4


def draw_medium_filter(key, part):
    key = jax.random.fold_in(key, 11)
    key_rate, key_noise = jax.random.split(key)
    log_span = jax.random.uniform(key_rate, (1, D), jnp.float32, math.log(10.0), math.log(3000.0))
    span = jnp.exp(log_span)
    lags = jnp.arange(FILT, dtype=jnp.float32)[:, None]
    decay = jnp.exp(-lags / span)
    ratio = jnp.exp(-2.0 / span)
    norm = jnp.sqrt((1.0 - ratio ** FILT) / (1.0 - ratio))
    noise = jax.random.truncated_normal(key_noise, -4.0, 4.0, (FILT, D), jnp.float32)
    return (noise * decay / norm).astype(jnp.bfloat16)


def strengthened(result, key, source, target, blocks, factor):
    owner, partner = [(jnp.arange(result.shape[axis_at]) // (result.shape[axis_at] // blocks)).reshape([-1 if axis == axis_at else 1 for axis in range(result.ndim)]) for axis_at in (source, target)]
    chosen = jax.random.permutation(key, blocks)[partner]
    strong = (owner == chosen) | (owner == (partner + blocks // 2) % blocks)
    return jnp.where(strong, factor * result, result)


def block_levels(key, dims, pieces, low, high):
    def one(dim, blocks):
        draws = jax.random.uniform(jax.random.fold_in(jax.random.fold_in(key, 6), dim), (blocks,), jnp.float32, low / len(pieces), high / len(pieces))
        return jnp.repeat(jnp.exp(draws), dims[dim] // blocks).reshape((-1,) + (1,) * (len(dims) - dim - 1))

    loudness = one(*pieces[0])
    for cut in pieces[1:]:
        loudness = loudness * one(*cut)
    return loudness


def bell_draw(own_key, dims, deviation, bound, cuts=(), held_as=jnp.bfloat16):
    array = deviation * jax.random.normal(own_key, dims, jnp.float32)
    if cuts:
        array = array * block_levels(own_key, dims, cuts, -0.22, 0.18)
    return jnp.clip(array, -bound, bound).astype(held_as)


def noise_with(own_key, dims, deviation, most, shards, heavy, held_as=jnp.bfloat16):
    values = deviation * jax.random.normal(own_key, dims, jnp.float32)
    if shards:
        values = values * block_levels(own_key, dims, shards, -0.22, 0.18)
    return jnp.clip(strengthened(values, jax.random.fold_in(own_key, 3), *heavy), -most, most).astype(held_as)


def setup_inputs(seed: int = 0) -> dict:
    seeds = jax.random.split(jax.random.key(seed), 7)
    streams = bell_draw(seeds[0], (3, TOKENS, D), 1.0, 6.0, ((1, 64), (2, 4)))
    residual_in = bell_draw(seeds[1], (TOKENS, D), 1.0, 6.0, ((0, 64), (1, 4)))
    short_filter = bell_draw(seeds[2], (3, SHORT, D), SHORT ** -0.5, 2.0, (), jnp.float32)
    medium_filter = draw_medium_filter(jax.random.fold_in(seeds[6], 71), 0)
    skip_gain = bell_draw(seeds[4], (D,), 1.0, 4.0, ((0, 4),), jnp.float32)
    w_out = noise_with(seeds[5], (D, D), D ** -0.5, 0.375, ((0, 256),), (0, 1, 256, 6.0))
    return {"streams": streams, "residual_in": residual_in, "short_filter": short_filter, "medium_filter": medium_filter, "skip_gain": skip_gain, "w_out": w_out}


def short_conv(extended, taps):
    length = extended.shape[1] - (SHORT - 1)
    total = jnp.zeros((extended.shape[0], length, extended.shape[2]), jnp.float32)
    for offset in range(SHORT):
        window = extended[:, SHORT - 1 - offset:SHORT - 1 - offset + length].astype(jnp.float32)
        total = total + taps[:, offset][:, None, :] * window
    return total


def reference(streams, residual_in, short_filter, medium_filter, skip_gain, w_out):
    reach = FILT - 1
    lead = reach + SHORT - 1
    padded = jnp.concatenate([jnp.zeros((3, lead, D), jnp.bfloat16), streams], axis=1)
    fft_len = 2 * TOK_DEV
    filter_spec = jnp.fft.rfft(medium_filter.astype(jnp.float32), n=fft_len, axis=0)
    group = D // N_CH

    def one_block(block_index):
        extended = lax.dynamic_slice_in_dim(padded, block_index * TOK_DEV, TOK_DEV + lead, 1)
        shorted = short_conv(extended, short_filter)
        query = shorted[0, reach:]
        product = (shorted[1] * shorted[2]).astype(jnp.bfloat16)
        product_f = product.astype(jnp.float32)
        spectrum = jnp.fft.rfft(product_f, n=fft_len, axis=0) * filter_spec
        mixed = jnp.fft.irfft(spectrum, n=fft_len, axis=0)[reach:reach + TOK_DEV]
        gated = (query * (mixed + skip_gain[None, :] * product_f[reach:])).astype(jnp.bfloat16)
        total = jnp.zeros((TOK_DEV, D), jnp.float32)
        for index in range(N_CH):
            part = jnp.dot(gated[:, index * group:(index + 1) * group], w_out[index * group:(index + 1) * group], preferred_element_type=jnp.float32).astype(jnp.bfloat16)
            part = lax.optimization_barrier(part)
            total = total + part.astype(jnp.float32)
        resid = lax.dynamic_slice_in_dim(residual_in, block_index * TOK_DEV, TOK_DEV, 0)
        return (total + resid.astype(jnp.float32)).astype(jnp.bfloat16)

    blocks = lax.map(one_block, jnp.arange(N_CTX, dtype=jnp.int32))
    return blocks.reshape(TOKENS, D)
```

```python
import functools

import jax
import jax.numpy as jnp
import numpy as np
from jax import lax
from jax.experimental import pallas as pl
from jax.experimental.pallas import tpu as pltpu
from jax.sharding import PartitionSpec as P

MESH = pl.DeviceIdType.MESH
NZ, NX, NC, NY = 8, 4, 2, 4
TOK = 256
CH = 1024
FILT = 128
SHORT = 7
ROWS = 16
WIN = FILT + TOK
HALF = WIN // 2
BLK = 256
CUT = 512


def transforms():
    freq = np.arange(HALF) + 0.5
    angle = 2 * np.pi * np.outer(freq, np.arange(WIN)) / WIN
    forward = np.concatenate([np.cos(angle), -np.sin(angle)], axis=0)
    inverse = forward.T[FILT:] * (2.0 / WIN)
    return forward, inverse


class Links:
    def __init__(self, send, recv):
        self.send, self.recv, self.count = send, recv, 0
        self.open = []

    def to(self, src, dst, device):
        copy = pltpu.make_async_remote_copy(
            src_ref=src,
            dst_ref=dst,
            send_sem=self.send.at[self.count],
            recv_sem=self.recv.at[self.count],
            device_id=device,
            device_id_type=MESH,
        )
        self.count += 1
        copy.start()
        self.open.append(copy)
        return copy

    def drain(self):
        for copy in self.open:
            copy.wait_send()


N_LINKS = 96
N_LOCAL = 10


def kernel(
    streams, residual, short, medium, skip, w_out, fwd, inv,
    out,
    sx, taps, med, gain, fwd_v, inv_v, res, prod, query, spec, wbuf, gbuf,
    send, recv, local,
):
    me, y = lax.axis_index("ctx"), lax.axis_index("ch")
    c = lax.rem(me, NC)
    x = lax.rem(me // NC, NX)
    z = me // (NC * NX)

    def at(zz, xx, cc):
        return (lax.rem(zz + NZ, NZ) * NX + lax.rem(xx + NX, NX)) * NC + cc

    def zmod(v):
        return lax.rem(v + NZ, NZ)

    def xmod(v):
        return lax.rem(v + NX, NX)

    def ymod(v):
        return lax.rem(v + NY, NY)

    n_ctx = NZ * NX * NC
    z_up, z_down = (at(z + 1, x, c), y), (at(z - 1, x, c), y)
    x_up, x_down = (at(z, x + 1, c), y), (at(z, x - 1, c), y)
    twin = (at(z, x, 1 - c), y)
    after, before = (lax.rem(me + 1, n_ctx), y), (lax.rem(me + n_ctx - 1, n_ctx), y)
    y_up, y_down, y_far = (me, ymod(y + 1)), (me, ymod(y - 1)), (me, ymod(y + 2))

    loads = []
    for i, (src, dst) in enumerate(
        (
            (medium, med),
            (fwd, fwd_v),
            (streams, sx.at[:, pl.ds(ROWS, TOK), :]),
            (short.at[:, :, pl.ds(pl.multiple_of(y * CH, CH), CH)], taps),
            (skip, gain),
            (inv, inv_v),
            (w_out.at[:, pl.ds(pl.multiple_of(y * CH, CH), CH)], wbuf.at[z, y, x, c]),
            (residual, res),
        )
    ):
        load = pltpu.make_async_copy(src, dst, local.at[i])
        load.start()
        loads.append(load)

    barrier = pltpu.get_barrier_semaphore()
    friends = (z_up, z_down, x_up, x_down, twin, after, before, y_up, y_down, y_far)
    for friend in friends:
        pl.semaphore_signal(barrier, inc=1, device_id=friend, device_id_type=MESH)

    loads[0].wait()
    loads[1].wait()

    def filter_spectrum(b, carry):
        lanes = pl.ds(pl.multiple_of(b * BLK, BLK), BLK)
        spec[:, lanes] = jnp.dot(
            fwd_v[:, 0:FILT], med[:, lanes], preferred_element_type=jnp.float32
        )
        return carry

    lax.fori_loop(0, CH // BLK, filter_spectrum, 0)

    pl.semaphore_wait(barrier, len(friends))

    links = Links(send, recv)

    spread = []
    for target, col in ((y_far, ymod(y + 2)), (y_up, ymod(y + 1)), (y_down, ymod(y - 1))):
        cols = pl.ds(pl.multiple_of(col * CH, CH), CH)
        spread.append(links.to(w_out.at[:, cols], wbuf.at[z, y, x, c], target))

    for load in loads[2:4]:
        load.wait()
    rim = links.to(sx.at[:, pl.ds(TOK, ROWS), :], sx.at[:, pl.ds(0, ROWS), :], after)

    def short_half(h):
        def lane_block(b, carry):
            lanes = pl.ds(pl.multiple_of(b * 128, 128), 128)
            rows = TOK // 2
            done = []
            for s in range(3):
                window = sx[s, pl.ds(h * rows, rows + ROWS), lanes].astype(jnp.float32)
                total = None
                for j in range(SHORT):
                    term = taps[s, j : j + 1, lanes] * window[ROWS - j : ROWS - j + rows]
                    total = term if total is None else total + term
                done.append(total)
            query[pl.ds(h * rows, rows), lanes] = done[0]
            prod[pl.ds(FILT + h * rows, rows), lanes] = (done[1] * done[2]).astype(jnp.bfloat16)
            return carry

        lax.fori_loop(0, CH // 128, lane_block, 0)

    short_half(1)
    rim_product = links.to(prod.at[pl.ds(TOK, FILT), :], prod.at[pl.ds(0, FILT), :], after)

    loads[6].wait()
    for copy in spread:
        copy.wait_recv()

    A, B = pl.ds(0, CUT), pl.ds(CUT, CH - CUT)

    def a_block(zz, xx):
        return wbuf.at[zz, :, xx, c, :, A]

    def b_block(xx):
        return wbuf.at[z, :, xx, c, :, B]

    def b_plane(zz):
        return wbuf.at[zz, :, :, c, :, B]

    def lower(kind, *place):
        zz = place[0] if kind != "bx" else z
        if kind == "a":
            return wbuf.at[zz, pl.ds(0, 2), place[1], c, :, A]
        if kind == "bx":
            return wbuf.at[zz, pl.ds(0, 2), place[0], c, :, B]
        return wbuf.at[zz, pl.ds(0, 2), :, c, :, B]

    def upper(kind, *place):
        zz = place[0] if kind != "bx" else z
        if kind == "a":
            return wbuf.at[zz, pl.ds(2, 2), place[1], c, :, A]
        if kind == "bx":
            return wbuf.at[zz, pl.ds(2, 2), place[0], c, :, B]
        return wbuf.at[zz, pl.ds(2, 2), :, c, :, B]

    def push(ref, device):
        return links.to(ref, ref, device)

    bx1 = [push(b_block(x), x_up), push(b_block(x), x_down)]
    az = [push(a_block(z, x), z_up), push(a_block(z, x), z_down)]
    ax1 = {0: [push(a_block(z, x), x_up), push(a_block(z, x), x_down)]}
    ax2 = {}

    rim.wait_recv()

    @pl.when(me == 0)
    def _():
        sx[:, 0:ROWS, :] = jnp.zeros((3, ROWS, CH), jnp.bfloat16)

    short_half(0)

    for copy in bx1:
        copy.wait_recv()
    bx2 = [push(lower("bx", xmod(x - 1)), x_up), push(upper("bx", xmod(x + 1)), x_down)]
    for copy in ax1[0]:
        copy.wait_recv()
    ax2[0] = [push(lower("a", z, xmod(x - 1)), x_up), push(upper("a", z, xmod(x + 1)), x_down)]

    rim_product.wait_recv()

    @pl.when(me == 0)
    def _():
        prod[0:FILT, :] = jnp.zeros((FILT, CH), jnp.bfloat16)

    loads[4].wait()
    loads[5].wait()

    def conv_block(b):
        lanes = pl.ds(b * BLK, BLK)
        freq = jnp.dot(fwd_v[...], prod[:, lanes], preferred_element_type=jnp.float32)
        fr, fi = freq[:HALF], freq[HALF:]
        hr, hi = spec[0:HALF, lanes], spec[HALF:WIN, lanes]
        both = jnp.concatenate([fr * hr - fi * hi, fr * hi + fi * hr], axis=0).astype(jnp.bfloat16)
        mixed = jnp.dot(inv_v[...], both, preferred_element_type=jnp.float32)
        direct = gain[0:1, lanes] * prod[pl.ds(FILT, TOK), lanes].astype(jnp.float32)
        gated = (query[:, lanes] * (mixed + direct)).astype(jnp.bfloat16)
        for part in range(BLK // 128):
            gbuf[y, b * (BLK // 128) + part] = gated[:, part * 128 : (part + 1) * 128]

    per = BLK // 128
    gy1, gy2 = {}, {}

    def send_gated(b):
        ref = gbuf.at[y, pl.ds(b * per, per)]
        gy1[b] = [push(ref, y_up), push(ref, y_down)]

    def forward_gated(b):
        for copy in gy1[b]:
            copy.wait_recv()
        low = gbuf.at[ymod(y - 1), pl.ds(b * per, per // 2)]
        high = gbuf.at[ymod(y + 1), pl.ds(b * per + per // 2, per // 2)]
        gy2[b] = [push(low, y_up), push(high, y_down)]

    conv_block(0)
    send_gated(0)
    for copy in bx2:
        copy.wait_recv()
    bz = [push(b_plane(z), z_up), push(b_plane(z), z_down)]

    conv_block(1)
    send_gated(1)

    planes = {0: (z,), 4: (zmod(z + 4),)}
    for s in range(1, 4):
        planes[s] = (zmod(z - s), zmod(z + s))
    siblings = []

    def start_ax1(s):
        copies = []
        for zz in planes[s]:
            copies += [push(a_block(zz, x), x_up), push(a_block(zz, x), x_down)]
        ax1[s] = copies

    def start_ax2(s):
        for copy in ax1[s]:
            copy.wait_recv()
        copies = []
        for zz in planes[s]:
            copies += [
                push(lower("a", zz, xmod(x - 1)), x_up),
                push(upper("a", zz, xmod(x + 1)), x_down),
            ]
        ax2[s] = copies

    def to_sibling(s):
        for copy in ax2[s]:
            copy.wait_recv()
        for zz in planes[s]:
            siblings.append(push(wbuf.at[zz, :, :, c], twin))

    def step_az(s):
        nonlocal az
        for copy in az:
            copy.wait_recv()
        if s < 3:
            az = [push(a_block(zmod(z - s), x), z_up), push(a_block(zmod(z + s), x), z_down)]
        elif s == 3:
            az = [push(lower("a", zmod(z - 3), x), z_up), push(upper("a", zmod(z + 3), x), z_down)]
        start_ax1(s)

    def step_bz(s):
        nonlocal bz
        for copy in bz:
            copy.wait_recv()
        if s < 3:
            bz = [push(b_plane(zmod(z - s)), z_up), push(b_plane(zmod(z + s)), z_down)]
        elif s == 3:
            bz = [push(lower("b", zmod(z - 3)), z_up), push(upper("b", zmod(z + 3)), z_down)]

    step_az(1)
    conv_block(2)
    send_gated(2)
    to_sibling(0)
    forward_gated(0)
    conv_block(3)
    send_gated(3)

    for s in range(1, 5):
        if s > 1:
            step_az(s)
        start_ax2(s)
        if s < 4:
            forward_gated(s)
        step_bz(s)
        to_sibling(s)

    for b in range(CH // BLK):
        for copy in gy2[b]:
            copy.wait_recv()
    for copy in siblings:
        copy.wait_recv()
    loads[7].wait()

    def project(n, carry):
        cols = pl.ds(pl.multiple_of(n * 256, 256), 256)
        total = res[:, cols].astype(jnp.float32)
        for zz in range(NZ):
            left = jnp.concatenate([gbuf[g, zz] for g in range(NY)], axis=1)
            right = wbuf[zz, :, :, :, :, cols].reshape(NY * 128, 256)
            total = total + jnp.dot(left, right, preferred_element_type=jnp.float32)
        out[:, cols] = total.astype(jnp.bfloat16)
        return carry

    lax.fori_loop(0, CH // 256, project, 0)
    links.drain()


def on_device(streams, residual_in, short_filter, medium_filter, skip_gain, w_out):
    forward, inverse = transforms()
    fwd = jnp.asarray(forward.astype(np.float32), dtype=jnp.bfloat16)
    inv = jnp.asarray(inverse.astype(np.float32), dtype=jnp.bfloat16)
    hbm = pl.BlockSpec(memory_space=pl.ANY)
    bf16, f32 = jnp.bfloat16, jnp.float32
    return pl.pallas_call(
        kernel,
        out_shape=jax.ShapeDtypeStruct((TOK, CH), bf16),
        in_specs=[hbm] * 8,
        out_specs=pl.BlockSpec(memory_space=pltpu.VMEM),
        scratch_shapes=[
            pltpu.VMEM((3, ROWS + TOK, CH), bf16),
            pltpu.VMEM((3, SHORT, CH), f32),
            pltpu.VMEM((FILT, CH), bf16),
            pltpu.VMEM((1, CH), f32),
            pltpu.VMEM((WIN, WIN), bf16),
            pltpu.VMEM((TOK, WIN), bf16),
            pltpu.VMEM((TOK, CH), bf16),
            pltpu.VMEM((WIN, CH), bf16),
            pltpu.VMEM((TOK, CH), f32),
            pltpu.VMEM((WIN, CH), f32),
            pltpu.VMEM((NZ, NY, NX, NC, ROWS, CH), bf16),
            pltpu.VMEM((NY, CH // 128, TOK, 128), bf16),
            pltpu.SemaphoreType.DMA((N_LINKS,)),
            pltpu.SemaphoreType.DMA((N_LINKS,)),
            pltpu.SemaphoreType.DMA((N_LOCAL,)),
        ],
        compiler_params=pltpu.CompilerParams(
            collective_id=0, has_side_effects=True, vmem_limit_bytes=40 * 1024 * 1024
        ),
    )(streams, residual_in, short_filter, medium_filter, skip_gain.reshape(1, CH), w_out, fwd, inv)


def solution(mesh):
    placed = (
        P(None, "ctx", "ch"),
        P("ctx", "ch"),
        P(),
        P(None, "ch"),
        P("ch"),
        P(("ch", "ctx"), None),
    )
    return jax.shard_map(
        on_device, mesh=mesh, in_specs=placed, out_specs=P("ctx", "ch"), check_vma=False
    )
```

```python
import functools

import jax
import jax.numpy as jnp
import numpy as np
from jax import lax
from jax.experimental import pallas as pl
from jax.experimental.pallas import tpu as pltpu
from jax.sharding import PartitionSpec as P

MESH = pl.DeviceIdType.MESH
NZ, NX, NC, NY = 8, 4, 2, 4
TOK = 256
CH = 1024
FILT = 128
SHORT = 7
ROWS = 16
WIN = FILT + TOK
HALF = WIN // 2
BLK = 256
CUT = 640
UP = 2
EDGE = FILT + ROWS
N_COPIES = 128


def transforms():
    freq = np.arange(HALF) + 0.5
    angle = 2 * np.pi * np.outer(freq, np.arange(WIN)) / WIN
    forward = np.concatenate([np.cos(angle), -np.sin(angle)], axis=0)
    inverse = forward.T[FILT:] * (2.0 / WIN)
    return forward, inverse


ORDER = (
    "s1", "em1u", "s3", "s2", "rim", "ex0u", "em1d", "sh1", "rimp", "sh0", "m1d", "m1u", "x0u", "o0", "spec", "ex0d",
    "fix", "x0d", "o2", "o1", "m2d", "x1u", "m2u", "x1d", "c1", "g1d", "g1u", "xx0u", "xx0d", "c0", "x7d", "g0d",
    "n1u", "n1d", "x7u", "g0u", "o3", "c3", "m3d", "xx1u", "m3u", "x2u", "x6d", "xx1d", "c2", "f1u", "g3u", "f1d",
    "x6u", "g2d", "xx7d", "n2u", "x2d", "g2u", "g3d", "h1d", "xx7u", "n2d", "m4u", "x3u", "x5d", "h0d", "m4d", "x3d",
    "xx6d", "f2u", "h1u", "f2d", "x5u", "xx6u", "xx2u", "t0", "h0u", "n3u", "n3d", "xx2d", "t7", "t1", "h2d", "x4d",
    "h2u", "x4u", "h3u", "h3d", "f3u", "f3d", "xx3d", "xx3u", "xx5u", "xx5d", "t6", "n4u", "n4d", "f4u", "t2",
    "xx4u", "xx4d", "f4d", "p0", "t3", "p7", "t5", "p1", "p6", "t4x", "t4z", "p2", "p5", "p3", "p4",
)
N_LOCAL = 9


def kernel(
    streams, residual, short, medium, skip, w_out, fwd_a, fwd_b, inv,
    out,
    sx, taps, med, gain, fwd_av, fwd_bv, inv_v, res, prod, query, spec, freq, wbuf, gbuf, acc,
    send, recv, local,
):
    me, y = lax.axis_index("ctx"), lax.axis_index("ch")
    c = lax.rem(me, NC)
    x = lax.rem(me // NC, NX)
    z = me // (NC * NX)

    def at(zz, xx, cc):
        return (lax.rem(zz + NZ, NZ) * NX + lax.rem(xx + NX, NX)) * NC + cc

    def ymod(v):
        return lax.rem(v + NY, NY)

    n_ctx = NZ * NX * NC
    z_to = {"u": (at(z + 1, x, c), y), "d": (at(z - 1, x, c), y)}
    x_to = {"u": (at(z, x + 1, c), y), "d": (at(z, x - 1, c), y)}
    y_to = {"u": (me, ymod(y + 1)), "d": (me, ymod(y - 1))}
    twin, y_far = (at(z, x, 1 - c), y), (me, ymod(y + 2))
    after, before = (lax.rem(me + 1, n_ctx), y), (lax.rem(me + n_ctx - 1, n_ctx), y)

    def owned(group):
        return pl.ds(pl.multiple_of(group * CH, CH), CH)

    loads = {}
    for i, (name, src, dst) in enumerate(
        (
            ("streams", streams, sx.at[:, pl.ds(ROWS, TOK), :]),
            ("short", short.at[:, :, owned(y)], taps),
            ("w_out", w_out.at[:, owned(y)], wbuf.at[0, c, 0, 0]),
            ("medium", medium, med),
            ("fwd_a", fwd_a, fwd_av),
            ("fwd_b", fwd_b, fwd_bv),
            ("skip", skip, gain),
            ("inv", inv, inv_v),
            ("residual", residual, res),
        )
    ):
        loads[name] = pltpu.make_async_copy(src, dst, local.at[i])
        loads[name].start()

    def loaded(*wanted):
        for name in wanted:
            if name in loads:
                loads.pop(name).wait()

    barrier = pltpu.get_barrier_semaphore()
    friends = (*z_to.values(), *x_to.values(), *y_to.values(), y_far, twin, after, before)
    for friend in friends:
        pl.semaphore_signal(barrier, inc=1, device_id=friend, device_id_type=MESH)
    pl.semaphore_wait(barrier, len(friends))

    moves = {}
    whole, x_cols, z_cols = pl.ds(0, CH), pl.ds(0, CUT), pl.ds(CUT, CH - CUT)
    every, rest = pl.ds(0, NY), pl.ds(1, NY - 1)
    half_z = {"u": pl.ds(0, 2), "d": pl.ds(2, 2)}
    half_x = {"u": pl.ds(0, UP), "d": pl.ds(UP, NY - UP)}
    own, near, far = pl.ds(0, 1), pl.ds(1, 2), pl.ds(3, 1)

    for k, device in ((1, y_to["u"]), (2, y_far), (3, y_to["d"])):
        moves[f"s{k}"] = (
            w_out.at[:, owned(ymod(y + k))], wbuf.at[0, c, 0, NY - k], device, ()
        )
    moves["rim"] = (streams.at[:, pl.ds(TOK - ROWS, ROWS), :], sx.at[:, pl.ds(0, ROWS), :], after, ())
    moves["rimp"] = (prod.at[pl.ds(TOK, FILT), :], prod.at[pl.ds(0, FILT), :], after, ("sh1",))

    def along_z(name, step, way, slots, groups, cols, needs):
        src = (1 - step) % NZ if way == "u" else step - 1
        dst = (src - 1) % NZ if way == "u" else src + 1
        moves[name] = (
            wbuf.at[src, c, slots, groups, :, cols],
            wbuf.at[dst, c, slots, groups, :, cols],
            z_to[way],
            needs,
        )

    def along_x(name, dz, way, src, dst, groups, cols, needs):
        moves[name] = (
            wbuf.at[dz, c, src, groups, :, cols], wbuf.at[dz, c, dst, groups, :, cols], x_to[way], needs
        )

    spread = ("s1", "s2", "s3")
    begun = ("x0u", "x0d", "ex0u", "ex0d")
    from_z = {0: begun, 4: ("m4u", "m4d")}
    for way in "ud":
        near_slot = 2 if way == "u" else 1
        mine = w_out.at[:, owned(y)]
        moves["em1" + way] = (mine, wbuf.at[7 if way == "u" else 1, c, 0, 0], z_to[way], ())
        along_z("m1" + way, 1, way, own, rest, whole, spread)
        moves["ex0" + way] = (mine, wbuf.at[0, c, near_slot, 0], x_to[way], ())
        along_x("x0" + way, 0, way, 0, near_slot, rest, whole, spread)
        for step in range(2, NZ // 2 + 1):
            last = step == NZ // 2
            groups = half_z[way] if last else every
            needs = ("m1" + way, "em1" + way) if step == 2 else (f"m{step - 1}{way}",)
            along_z(f"m{step}{way}", step, way, own, groups, whole, needs)
            along_z(f"n{step}{way}", step, way, near, groups, z_cols, (f"n{step - 1}{way}",))
            along_z(f"f{step}{way}", step, way, far, groups, z_cols, (f"f{step - 1}{way}",))
        along_z("n1" + way, 1, way, near, every, z_cols, begun)
        along_z("f1" + way, 1, way, far, every, z_cols, ("xx0u", "xx0d"))
        for dz in range(NZ):
            if dz not in from_z:
                step = min(dz, NZ - dz)
                ways = "d" if dz < NZ // 2 else "u"
                from_z[dz] = tuple(f"{kind}{step}{ways}" for kind in ("m", "em")[: 2 if step == 1 else 1])
            cols = x_cols if dz else whole
            if dz:
                along_x(f"x{dz}{way}", dz, way, 0, near_slot, every, cols, from_z[dz])
            needs = (f"x{dz}{way}",) if dz else ("x0" + way, "ex0" + way)
            along_x(f"xx{dz}{way}", dz, way, near_slot, 3, half_x[way], cols, needs)
        for b in range(CH // BLK):
            per = BLK // 128
            chunk = pl.ds(b * per, per)
            half = pl.ds(b * per + (0 if way == "u" else per // 2), per // 2)
            group = 3 if way == "u" else 1
            moves[f"g{b}{way}"] = (gbuf.at[0, chunk], gbuf.at[group, chunk], y_to[way], (f"c{b}",))
            moves[f"h{b}{way}"] = (gbuf.at[group, half], gbuf.at[2, half], y_to[way], (f"g{b}{way}",))
    for dz in range(NZ):
        by_x = from_z[dz] + tuple(f"{kind}{dz}{way}" for kind in ("x", "xx") for way in "ud")
        step = min(dz, NZ - dz)
        ways = "ud" if dz == NZ // 2 else "d" if dz < NZ // 2 else "u"
        by_z = tuple(f"{kind}{step}{way}" for kind in ("n", "f") for way in ways) if dz else ()
        if dz == 0:
            by_x = ("own",) + spread + by_x
        if dz == NZ // 2:
            for name, cols, needs in (("t4x", x_cols, by_x), ("t4z", z_cols, by_z + from_z[dz])):
                part = wbuf.at[dz, c, :, :, :, cols]
                moves[name] = (part, part, twin, needs)
        else:
            moves[f"t{dz}"] = (wbuf.at[dz, c], wbuf.at[dz, c], twin, by_x + by_z)

    def short_rows(start, rows):
        def lane_block(b, carry):
            lanes = pl.ds(pl.multiple_of(b * 128, 128), 128)
            done = []
            for s in range(3):
                window = sx[s, pl.ds(start, rows + ROWS), lanes].astype(jnp.float32)
                total = None
                for j in range(SHORT):
                    term = taps[s, j : j + 1, lanes] * window[ROWS - j : ROWS - j + rows]
                    total = term if total is None else total + term
                done.append(total)
            query[pl.ds(start, rows), lanes] = done[0]
            prod[pl.ds(FILT + start, rows), lanes] = (done[1] * done[2]).astype(jnp.bfloat16)
            return carry

        lax.fori_loop(0, CH // 128, lane_block, 0)

    def short_last():
        loaded("streams", "short")
        short_rows(FILT, FILT)

    def short_first():
        short_rows(ROWS, FILT - ROWS)

    def short_edge():
        @pl.when(me == 0)
        def _():
            sx[:, 0:ROWS, :] = jnp.zeros((3, ROWS, CH), jnp.bfloat16)

        short_rows(0, ROWS)

    def filter_spectrum():
        loaded("medium", "fwd_a")

        def body(b, carry):
            lanes = pl.ds(pl.multiple_of(b * BLK, BLK), BLK)
            spec[:, lanes] = jnp.dot(
                fwd_av[:, 0:FILT], med[:, lanes], preferred_element_type=jnp.float32
            )
            return carry

        lax.fori_loop(0, CH // BLK, body, 0)

    def own_spectrum(b):
        loaded("fwd_b")
        lanes = pl.ds(b * BLK, BLK)
        freq[:, lanes] = jnp.dot(
            fwd_bv[...], prod[EDGE:WIN, lanes], preferred_element_type=jnp.float32
        )

    edge_ready = []

    def conv_block(b):
        loaded("skip", "inv")
        if not edge_ready:
            edge_ready.append(b)

            @pl.when(me == 0)
            def _():
                prod[0:FILT, :] = jnp.zeros((FILT, CH), jnp.bfloat16)

        lanes = pl.ds(b * BLK, BLK)
        total = freq[:, lanes] + jnp.dot(
            fwd_av[...], prod[0:EDGE, lanes], preferred_element_type=jnp.float32
        )
        fr, fi = total[:HALF], total[HALF:]
        hr, hi = spec[0:HALF, lanes], spec[HALF:WIN, lanes]
        both = jnp.concatenate([fr * hr - fi * hi, fr * hi + fi * hr], axis=0).astype(jnp.bfloat16)
        mixed = jnp.dot(inv_v[...], both, preferred_element_type=jnp.float32)
        direct = gain[0:1, lanes] * prod[pl.ds(FILT, TOK), lanes].astype(jnp.float32)
        gated = (query[:, lanes] * (mixed + direct)).astype(jnp.bfloat16)
        for part in range(BLK // 128):
            gbuf[0, b * (BLK // 128) + part] = gated[:, part * 128 : (part + 1) * 128]

    projected = []

    def project(dz):
        loaded("residual")
        begin, end = not projected, len(projected) == NZ - 1
        projected.append(dz)
        plane = lax.rem(z + dz, NZ)

        def body(n, carry):
            cols = pl.ds(pl.multiple_of(n * 256, 256), 256)
            total = res[:, cols].astype(jnp.float32) if begin else acc[:, cols]
            left = jnp.concatenate([gbuf[g, plane] for g in range(NY)], axis=1)
            pieces = []
            for g in range(NY):
                for xx in range(NX):
                    dx = lax.rem(xx - x + NX, NX)
                    slot = dx + dx // 2 - 2 * (dx // 3)
                    pieces += [wbuf[dz, cc, slot, g, :, cols] for cc in range(NC)]
            right = jnp.concatenate(pieces, axis=0)
            total = total + jnp.dot(left, right, preferred_element_type=jnp.float32)
            if end:
                out[:, cols] = total.astype(jnp.bfloat16)
            else:
                acc[:, cols] = total
            return carry

        lax.fori_loop(0, CH // 256, body, 0)

    tasks = {
        "sh1": (short_last, ()),
        "sh0": (short_first, ()),
        "spec": (filter_spectrum, ()),
        "fix": (short_edge, ("rim", "sh1")),
    }
    for b in range(CH // BLK):
        tasks[f"o{b}"] = (functools.partial(own_spectrum, b), ("sh1", "sh0"))
        tasks[f"c{b}"] = (functools.partial(conv_block, b), ("rimp", "fix", "spec", f"o{b}"))
    gated_all = tuple(f"{kind}{b}{way}" for kind in "gh" for b in range(CH // BLK) for way in "ud")
    for dz in range(NZ):
        twins = (f"t{dz}",) if dz != NZ // 2 else ("t4x", "t4z")
        tasks[f"p{dz}"] = (functools.partial(project, dz), twins + gated_all)

    copies, seen, ran = {}, set(), set()

    def await_all(needs):
        for name in needs:
            if name == "own":
                loaded("w_out")
            elif name in tasks:
                assert name in ran
            elif name not in seen:
                seen.add(name)
                copies[name].wait_recv()

    assert sorted(ORDER) == sorted([*moves, *tasks])
    for name in ORDER:
        if name in tasks:
            task, needs = tasks[name]
            await_all(needs)
            task()
            ran.add(name)
            continue
        src, dst, device, needs = moves[name]
        await_all(needs)
        i = len(copies)
        copies[name] = pltpu.make_async_remote_copy(
            src_ref=src,
            dst_ref=dst,
            send_sem=send.at[i],
            recv_sem=recv.at[i],
            device_id=device,
            device_id_type=MESH,
        )
        copies[name].start()
    await_all(copies)
    for copy in copies.values():
        copy.wait_send()


def on_device(streams, residual_in, short_filter, medium_filter, skip_gain, w_out):
    forward, inverse = transforms()
    fwd_a = jnp.asarray(forward[:, :EDGE].astype(np.float32), dtype=jnp.bfloat16)
    fwd_b = jnp.asarray(forward[:, EDGE:].astype(np.float32), dtype=jnp.bfloat16)
    inv = jnp.asarray(inverse.astype(np.float32), dtype=jnp.bfloat16)
    hbm = pl.BlockSpec(memory_space=pl.ANY)
    bf16, f32 = jnp.bfloat16, jnp.float32
    return pl.pallas_call(
        kernel,
        out_shape=jax.ShapeDtypeStruct((TOK, CH), bf16),
        in_specs=[hbm] * 9,
        out_specs=pl.BlockSpec(memory_space=pltpu.VMEM),
        scratch_shapes=[
            pltpu.VMEM((3, ROWS + TOK, CH), bf16),
            pltpu.VMEM((3, SHORT, CH), f32),
            pltpu.VMEM((FILT, CH), bf16),
            pltpu.VMEM((1, CH), f32),
            pltpu.VMEM((WIN, EDGE), bf16),
            pltpu.VMEM((WIN, WIN - EDGE), bf16),
            pltpu.VMEM((TOK, WIN), bf16),
            pltpu.VMEM((TOK, CH), bf16),
            pltpu.VMEM((WIN, CH), bf16),
            pltpu.VMEM((TOK, CH), f32),
            pltpu.VMEM((WIN, CH), f32),
            pltpu.VMEM((WIN, CH), f32),
            pltpu.VMEM((NZ, NC, NX, NY, ROWS, CH), bf16),
            pltpu.VMEM((NY, CH // 128, TOK, 128), bf16),
            pltpu.VMEM((TOK, CH), f32),
            pltpu.SemaphoreType.DMA((N_COPIES,)),
            pltpu.SemaphoreType.DMA((N_COPIES,)),
            pltpu.SemaphoreType.DMA((N_LOCAL,)),
        ],
        compiler_params=pltpu.CompilerParams(
            collective_id=0, has_side_effects=True, vmem_limit_bytes=63 * 1024 * 1024
        ),
    )(streams, residual_in, short_filter, medium_filter, skip_gain.reshape(1, CH), w_out, fwd_a, fwd_b, inv)


def solution(mesh):
    placed = (
        P(None, "ctx", "ch"),
        P("ctx", "ch"),
        P(),
        P(None, "ch"),
        P("ch"),
        P(("ch", "ctx"), None),
    )
    return jax.shard_map(
        on_device, mesh=mesh, in_specs=placed, out_specs=P("ctx", "ch"), check_vma=False
    )
```

```python
import functools

import jax
import jax.numpy as jnp
import numpy as np
from jax import lax
from jax.experimental import pallas as pl
from jax.experimental.pallas import tpu as pltpu
from jax.sharding import PartitionSpec as P

MESH = pl.DeviceIdType.MESH
NZ, NX, NC, NY = 8, 4, 2, 4
TOK = 256
CH = 1024
FILT = 128
SHORT = 7
ROWS = 16
WIN = FILT + TOK
HALF = WIN // 2
BLK = 256
CUT = 640
UP = 2
LESS_UP = ()
EDGE = FILT + ROWS
N_COPIES = 128


def transforms():
    freq = np.arange(HALF) + 0.5
    angle = 2 * np.pi * np.outer(freq, np.arange(WIN)) / WIN
    forward = np.concatenate([np.cos(angle), -np.sin(angle)], axis=0)
    inverse = forward.T[FILT:] * (2.0 / WIN)
    return forward, inverse


ORDER = (
    "s1", "rim", "em1d", "s3", "s2", "em1u", "sh1", "rimp", "m1u", "x0d", "m1d", "ex0u", "sh0", "ex0d", "x0u", "o2",
    "fix", "spec", "o0", "o1", "m2u", "x1d", "x7u", "m2d", "x1u", "x7d", "c0", "xx0d", "g0d", "n1u", "xx0u", "n1d",
    "g0u", "c1", "c2", "g2u", "xx1d", "x6u", "x6d", "g2d", "m3d", "g1d", "m3u", "xx7u", "o3", "x2d", "h0u", "xx1u",
    "g1u", "xx7d", "f1d", "f1u", "x2u", "c3", "n2d", "n2u", "m4d", "m4u", "xx6u", "g3d", "x3d", "t0", "xx6d", "x5u",
    "g3u", "f2d", "f2u", "h2d", "h2u", "x3u", "x5d", "h0d", "n3d", "n3u", "h1d", "x4u", "x4d", "xx2u", "xx2d", "h3d",
    "t7", "h1u", "f3d", "f3u", "xx3u", "t6", "t1", "xx5u", "xx3d", "xx5d", "h3u", "n4u", "n4d", "xx4u", "xx4d",
    "f4u", "f4d", "t2", "t3", "p0", "t5", "p7", "p1", "t4x", "t4z", "p6", "p2", "p5", "p3", "p4",
)
N_LOCAL = 9


def kernel(
    streams, residual, short, medium, skip, w_out, fwd_a, fwd_b, inv,
    out,
    sx, taps, med, gain, fwd_av, fwd_bv, inv_v, res, prod, query, spec, freq, wbuf, gbuf, acc,
    send, recv, local,
):
    me, y = lax.axis_index("ctx"), lax.axis_index("ch")
    c = lax.rem(me, NC)
    x = lax.rem(me // NC, NX)
    z = me // (NC * NX)

    def at(zz, xx, cc):
        return (lax.rem(zz + NZ, NZ) * NX + lax.rem(xx + NX, NX)) * NC + cc

    def ymod(v):
        return lax.rem(v + NY, NY)

    n_ctx = NZ * NX * NC
    z_to = {"u": (at(z + 1, x, c), y), "d": (at(z - 1, x, c), y)}
    x_to = {"u": (at(z, x + 1, c), y), "d": (at(z, x - 1, c), y)}
    y_to = {"u": (me, ymod(y + 1)), "d": (me, ymod(y - 1))}
    twin, y_far = (at(z, x, 1 - c), y), (me, ymod(y + 2))
    after, before = (lax.rem(me + 1, n_ctx), y), (lax.rem(me + n_ctx - 1, n_ctx), y)

    def owned(group):
        return pl.ds(pl.multiple_of(group * CH, CH), CH)

    loads = {}
    for i, (name, src, dst) in enumerate(
        (
            ("streams", streams, sx.at[:, pl.ds(ROWS, TOK), :]),
            ("short", short.at[:, :, owned(y)], taps),
            ("w_out", w_out.at[:, owned(y)], wbuf.at[0, c, 0, 0]),
            ("medium", medium, med),
            ("fwd_a", fwd_a, fwd_av),
            ("fwd_b", fwd_b, fwd_bv),
            ("skip", skip, gain),
            ("inv", inv, inv_v),
            ("residual", residual, res),
        )
    ):
        loads[name] = pltpu.make_async_copy(src, dst, local.at[i])
        loads[name].start()

    def loaded(*wanted):
        for name in wanted:
            if name in loads:
                loads.pop(name).wait()

    barrier = pltpu.get_barrier_semaphore()
    friends = (*z_to.values(), *x_to.values(), *y_to.values(), y_far, twin, after, before)
    for friend in friends:
        pl.semaphore_signal(barrier, inc=1, device_id=friend, device_id_type=MESH)
    pl.semaphore_wait(barrier, len(friends))

    moves = {}
    whole, x_cols, z_cols = pl.ds(0, CH), pl.ds(0, CUT), pl.ds(CUT, CH - CUT)
    every, rest = pl.ds(0, NY), pl.ds(1, NY - 1)
    half_z = {"u": pl.ds(0, 2), "d": pl.ds(2, 2)}

    def half_x(dz, way):
        groups = UP - 1 if dz in LESS_UP else UP
        return pl.ds(0, groups) if way == "u" else pl.ds(groups, NY - groups)

    own, near, far = pl.ds(0, 1), pl.ds(1, 2), pl.ds(3, 1)

    for k, device in ((1, y_to["u"]), (2, y_far), (3, y_to["d"])):
        moves[f"s{k}"] = (
            w_out.at[:, owned(ymod(y + k))], wbuf.at[0, c, 0, NY - k], device, ()
        )
    moves["rim"] = (streams.at[:, pl.ds(TOK - ROWS, ROWS), :], sx.at[:, pl.ds(0, ROWS), :], after, ())
    moves["rimp"] = (prod.at[pl.ds(TOK, FILT), :], prod.at[pl.ds(0, FILT), :], after, ("sh1",))

    def along_z(name, step, way, slots, groups, cols, needs):
        src = (1 - step) % NZ if way == "u" else step - 1
        dst = (src - 1) % NZ if way == "u" else src + 1
        moves[name] = (
            wbuf.at[src, c, slots, groups, :, cols],
            wbuf.at[dst, c, slots, groups, :, cols],
            z_to[way],
            needs,
        )

    def along_x(name, dz, way, src, dst, groups, cols, needs):
        moves[name] = (
            wbuf.at[dz, c, src, groups, :, cols], wbuf.at[dz, c, dst, groups, :, cols], x_to[way], needs
        )

    spread = ("s1", "s2", "s3")
    begun = ("x0u", "x0d", "ex0u", "ex0d")
    from_z = {0: begun, 4: ("m4u", "m4d")}
    for way in "ud":
        near_slot = 2 if way == "u" else 1
        mine = w_out.at[:, owned(y)]
        moves["em1" + way] = (mine, wbuf.at[7 if way == "u" else 1, c, 0, 0], z_to[way], ())
        along_z("m1" + way, 1, way, own, rest, whole, spread)
        moves["ex0" + way] = (mine, wbuf.at[0, c, near_slot, 0], x_to[way], ())
        along_x("x0" + way, 0, way, 0, near_slot, rest, whole, spread)
        for step in range(2, NZ // 2 + 1):
            last = step == NZ // 2
            groups = half_z[way] if last else every
            needs = ("m1" + way, "em1" + way) if step == 2 else (f"m{step - 1}{way}",)
            along_z(f"m{step}{way}", step, way, own, groups, whole, needs)
            along_z(f"n{step}{way}", step, way, near, groups, z_cols, (f"n{step - 1}{way}",))
            along_z(f"f{step}{way}", step, way, far, groups, z_cols, (f"f{step - 1}{way}",))
        along_z("n1" + way, 1, way, near, every, z_cols, begun)
        along_z("f1" + way, 1, way, far, every, z_cols, ("xx0u", "xx0d"))
        for dz in range(NZ):
            if dz not in from_z:
                step = min(dz, NZ - dz)
                ways = "d" if dz < NZ // 2 else "u"
                from_z[dz] = tuple(f"{kind}{step}{ways}" for kind in ("m", "em")[: 2 if step == 1 else 1])
            cols = x_cols if dz else whole
            if dz:
                along_x(f"x{dz}{way}", dz, way, 0, near_slot, every, cols, from_z[dz])
            needs = (f"x{dz}{way}",) if dz else ("x0" + way, "ex0" + way)
            along_x(f"xx{dz}{way}", dz, way, near_slot, 3, half_x(dz, way), cols, needs)
        for b in range(CH // BLK):
            per = BLK // 128
            chunk = pl.ds(b * per, per)
            half = pl.ds(b * per + (0 if way == "u" else per // 2), per // 2)
            group = 3 if way == "u" else 1
            moves[f"g{b}{way}"] = (gbuf.at[0, chunk], gbuf.at[group, chunk], y_to[way], (f"c{b}",))
            moves[f"h{b}{way}"] = (gbuf.at[group, half], gbuf.at[2, half], y_to[way], (f"g{b}{way}",))
    for dz in range(NZ):
        by_x = from_z[dz] + tuple(f"{kind}{dz}{way}" for kind in ("x", "xx") for way in "ud")
        step = min(dz, NZ - dz)
        ways = "ud" if dz == NZ // 2 else "d" if dz < NZ // 2 else "u"
        by_z = tuple(f"{kind}{step}{way}" for kind in ("n", "f") for way in ways) if dz else ()
        if dz == 0:
            by_x = ("own",) + spread + by_x
        if dz == NZ // 2:
            for name, cols, needs in (("t4x", x_cols, by_x), ("t4z", z_cols, by_z + from_z[dz])):
                part = wbuf.at[dz, c, :, :, :, cols]
                moves[name] = (part, part, twin, needs)
        else:
            moves[f"t{dz}"] = (wbuf.at[dz, c], wbuf.at[dz, c], twin, by_x + by_z)

    def short_rows(start, rows):
        def lane_block(b, carry):
            lanes = pl.ds(pl.multiple_of(b * 128, 128), 128)
            done = []
            for s in range(3):
                window = sx[s, pl.ds(start, rows + ROWS), lanes].astype(jnp.float32)
                total = None
                for j in range(SHORT):
                    term = taps[s, j : j + 1, lanes] * window[ROWS - j : ROWS - j + rows]
                    total = term if total is None else total + term
                done.append(total)
            query[pl.ds(start, rows), lanes] = done[0]
            prod[pl.ds(FILT + start, rows), lanes] = (done[1] * done[2]).astype(jnp.bfloat16)
            return carry

        lax.fori_loop(0, CH // 128, lane_block, 0)

    def short_last():
        loaded("streams", "short")
        short_rows(FILT, FILT)

    def short_first():
        short_rows(ROWS, FILT - ROWS)

    def short_edge():
        @pl.when(me == 0)
        def _():
            sx[:, 0:ROWS, :] = jnp.zeros((3, ROWS, CH), jnp.bfloat16)

        short_rows(0, ROWS)

    def filter_spectrum():
        loaded("medium", "fwd_a")

        for b in range(CH // BLK):
            lanes = pl.ds(b * BLK, BLK)
            spec[:, lanes] = jnp.dot(
                fwd_av[:, 0:FILT], med[:, lanes], preferred_element_type=jnp.float32
            )

    def own_spectrum(b):
        loaded("fwd_b")
        lanes = pl.ds(b * BLK, BLK)
        freq[:, lanes] = jnp.dot(
            fwd_bv[...], prod[EDGE:WIN, lanes], preferred_element_type=jnp.float32
        )

    edge_ready = []

    def conv_block(b):
        loaded("skip", "inv")
        if not edge_ready:
            edge_ready.append(b)

            @pl.when(me == 0)
            def _():
                prod[0:FILT, :] = jnp.zeros((FILT, CH), jnp.bfloat16)

        lanes = pl.ds(b * BLK, BLK)
        total = freq[:, lanes] + jnp.dot(
            fwd_av[...], prod[0:EDGE, lanes], preferred_element_type=jnp.float32
        )
        fr, fi = total[:HALF], total[HALF:]
        hr, hi = spec[0:HALF, lanes], spec[HALF:WIN, lanes]
        both = jnp.concatenate([fr * hr - fi * hi, fr * hi + fi * hr], axis=0).astype(jnp.bfloat16)
        mixed = jnp.dot(inv_v[...], both, preferred_element_type=jnp.float32)
        direct = gain[0:1, lanes] * prod[pl.ds(FILT, TOK), lanes].astype(jnp.float32)
        gated = (query[:, lanes] * (mixed + direct)).astype(jnp.bfloat16)
        for part in range(BLK // 128):
            gbuf[0, b * (BLK // 128) + part] = gated[:, part * 128 : (part + 1) * 128]

    projected = []

    def project(dz):
        loaded("residual")
        begin, end = not projected, len(projected) == NZ - 1
        projected.append(dz)
        plane = lax.rem(z + dz, NZ)

        left = jnp.concatenate([gbuf[g, plane] for g in range(NY)], axis=1)
        for n in range(CH // BLK):
            cols = pl.ds(n * BLK, BLK)
            pieces = []
            for g in range(NY):
                for xx in range(NX):
                    dx = lax.rem(xx - x + NX, NX)
                    slot = dx + dx // 2 - 2 * (dx // 3)
                    pieces += [wbuf[dz, cc, slot, g, :, cols] for cc in range(NC)]
            right = jnp.concatenate(pieces, axis=0)
            total = res[:, cols].astype(jnp.float32) if begin else acc[:, cols]
            total = total + jnp.dot(left, right, preferred_element_type=jnp.float32)
            if end:
                out[:, cols] = total.astype(jnp.bfloat16)
            else:
                acc[:, cols] = total

    tasks = {
        "sh1": (short_last, ()),
        "sh0": (short_first, ()),
        "spec": (filter_spectrum, ()),
        "fix": (short_edge, ("rim", "sh1")),
    }
    for b in range(CH // BLK):
        tasks[f"o{b}"] = (functools.partial(own_spectrum, b), ("sh1", "sh0"))
        tasks[f"c{b}"] = (functools.partial(conv_block, b), ("rimp", "fix", "spec", f"o{b}"))
    gated_all = tuple(f"{kind}{b}{way}" for kind in "gh" for b in range(CH // BLK) for way in "ud")
    for dz in range(NZ):
        twins = (f"t{dz}",) if dz != NZ // 2 else ("t4x", "t4z")
        tasks[f"p{dz}"] = (functools.partial(project, dz), twins + gated_all)

    copies, seen, ran = {}, set(), set()

    def await_all(needs):
        for name in needs:
            if name == "own":
                loaded("w_out")
            elif name in tasks:
                assert name in ran
            elif name not in seen:
                seen.add(name)
                copies[name].wait_recv()

    assert sorted(ORDER) == sorted([*moves, *tasks])
    for name in ORDER:
        if name in tasks:
            task, needs = tasks[name]
            await_all(needs)
            task()
            ran.add(name)
            continue
        src, dst, device, needs = moves[name]
        await_all(needs)
        i = len(copies)
        copies[name] = pltpu.make_async_remote_copy(
            src_ref=src,
            dst_ref=dst,
            send_sem=send.at[i],
            recv_sem=recv.at[i],
            device_id=device,
            device_id_type=MESH,
        )
        copies[name].start()
    await_all(copies)
    for copy in copies.values():
        copy.wait_send()


def on_device(streams, residual_in, short_filter, medium_filter, skip_gain, w_out):
    forward, inverse = transforms()
    fwd_a = jnp.asarray(forward[:, :EDGE].astype(np.float32), dtype=jnp.bfloat16)
    fwd_b = jnp.asarray(forward[:, EDGE:].astype(np.float32), dtype=jnp.bfloat16)
    inv = jnp.asarray(inverse.astype(np.float32), dtype=jnp.bfloat16)
    hbm = pl.BlockSpec(memory_space=pl.ANY)
    bf16, f32 = jnp.bfloat16, jnp.float32
    return pl.pallas_call(
        kernel,
        out_shape=jax.ShapeDtypeStruct((TOK, CH), bf16),
        in_specs=[hbm] * 9,
        out_specs=pl.BlockSpec(memory_space=pltpu.VMEM),
        scratch_shapes=[
            pltpu.VMEM((3, ROWS + TOK, CH), bf16),
            pltpu.VMEM((3, SHORT, CH), f32),
            pltpu.VMEM((FILT, CH), bf16),
            pltpu.VMEM((1, CH), f32),
            pltpu.VMEM((WIN, EDGE), bf16),
            pltpu.VMEM((WIN, WIN - EDGE), bf16),
            pltpu.VMEM((TOK, WIN), bf16),
            pltpu.VMEM((TOK, CH), bf16),
            pltpu.VMEM((WIN, CH), bf16),
            pltpu.VMEM((TOK, CH), f32),
            pltpu.VMEM((WIN, CH), f32),
            pltpu.VMEM((WIN, CH), f32),
            pltpu.VMEM((NZ, NC, NX, NY, ROWS, CH), bf16),
            pltpu.VMEM((NY, CH // 128, TOK, 128), bf16),
            pltpu.VMEM((TOK, CH), f32),
            pltpu.SemaphoreType.DMA((N_COPIES,)),
            pltpu.SemaphoreType.DMA((N_COPIES,)),
            pltpu.SemaphoreType.DMA((N_LOCAL,)),
        ],
        compiler_params=pltpu.CompilerParams(
            collective_id=0, has_side_effects=True, vmem_limit_bytes=63 * 1024 * 1024
        ),
    )(streams, residual_in, short_filter, medium_filter, skip_gain.reshape(1, CH), w_out, fwd_a, fwd_b, inv)


def solution(mesh):
    placed = (
        P(None, "ctx", "ch"),
        P("ctx", "ch"),
        P(),
        P(None, "ch"),
        P("ch"),
        P(("ch", "ctx"), None),
    )
    return jax.shard_map(
        on_device, mesh=mesh, in_specs=placed, out_specs=P("ctx", "ch"), check_vma=False
    )
```

```python
import functools

import jax
import jax.numpy as jnp
import numpy as np
from jax import lax
from jax.experimental import pallas as pl
from jax.experimental.pallas import tpu as pltpu
from jax.sharding import PartitionSpec as P

MESH = pl.DeviceIdType.MESH
NZ, NX, NC, NY = 8, 4, 2, 4
TOK = 256
CH = 1024
FILT = 128
SHORT = 7
ROWS = 16
WIN = FILT + TOK
HALF = WIN // 2
BLK = 256
CUT = 640
UP = 2
LESS_UP = ()
EDGE = FILT + ROWS
N_COPIES = 128


def transforms():
    freq = np.arange(HALF) + 0.5
    angle = 2 * np.pi * np.outer(freq, np.arange(WIN)) / WIN
    forward = np.concatenate([np.cos(angle), -np.sin(angle)], axis=0)
    inverse = forward.T[FILT:] * (2.0 / WIN)
    return forward, inverse


ORDER = (
    "s2", "ex0u", "s1", "rim", "s3", "sh1", "rimp", "em1d", "em1u", "m1d", "m1u", "spec", "x0d", "ex0d", "x0u",
    "sh0", "o2", "o0", "m2d", "x1u", "x1d", "m2u", "x7d", "fix", "x7u", "c0", "n1d", "n1u", "g0u", "xx0u", "g0d",
    "xx0d", "c2", "o3", "m3d", "x2u", "g2u", "g2d", "x2d", "x6u", "m3u", "xx7d", "o1", "xx7u", "x6d", "c1", "g1d",
    "f1d", "f1u", "n2d", "g1u", "xx1u", "c3", "n2u", "m4d", "x3d", "xx2d", "h0u", "g3u", "g3d", "m4u", "h0d", "x3u",
    "xx2u", "x5u", "xx1d", "f2u", "f2d", "x5d", "n3u", "n3d", "x4d", "x4u", "xx6d", "h2d", "h1u", "xx6u", "f3u",
    "xx3u", "xx3d", "f3d", "h1d", "t1", "h2u", "xx5u", "h3d", "t0", "h3u", "xx5d", "t7", "t2", "n4d", "n4u", "xx4d",
    "xx4u", "f4u", "t6", "f4d", "t3", "t5", "p0", "p7", "t4x", "p1", "t4z", "p6", "p2", "p5", "p3", "p4x", "p4",
)
N_LOADS = 10


def kernel(
    streams, residual, short, medium, skip, w_out, fwd_a, fwd_b, inv,
    result,
    sx, taps, med, gain, fwd_av, fwd_bv, inv_v, res, prod, query, spec, freq, wbuf, gbuf, acc, out, w_rows,
    send, recv, local,
):
    me, y = lax.axis_index("ctx"), lax.axis_index("ch")
    c = lax.rem(me, NC)
    x = lax.rem(me // NC, NX)
    z = me // (NC * NX)

    def at(zz, xx, cc):
        return (lax.rem(zz + NZ, NZ) * NX + lax.rem(xx + NX, NX)) * NC + cc

    def ymod(v):
        return lax.rem(v + NY, NY)

    n_ctx = NZ * NX * NC
    z_to = {"u": (at(z + 1, x, c), y), "d": (at(z - 1, x, c), y)}
    x_to = {"u": (at(z, x + 1, c), y), "d": (at(z, x - 1, c), y)}
    y_to = {"u": (me, ymod(y + 1)), "d": (me, ymod(y - 1))}
    twin, y_far = (at(z, x, 1 - c), y), (me, ymod(y + 2))
    after, before = (lax.rem(me + 1, n_ctx), y), (lax.rem(me + n_ctx - 1, n_ctx), y)

    def owned(group):
        return pl.ds(pl.multiple_of(group * CH, CH), CH)

    loads = {}
    for i, (name, src, dst) in enumerate(
        (
            ("w_rows", w_out, w_rows),
            ("streams", streams, sx.at[:, pl.ds(ROWS, TOK), :]),
            ("short", short.at[:, :, owned(y)], taps),
            ("w_out", w_out.at[:, owned(y)], wbuf.at[0, c, 0, 0]),
            ("medium", medium, med),
            ("fwd_a", fwd_a, fwd_av),
            ("fwd_b", fwd_b, fwd_bv),
            ("skip", skip, gain),
            ("inv", inv, inv_v),
            ("residual", residual, res),
        )
    ):
        loads[name] = pltpu.make_async_copy(src, dst, local.at[i])
        loads[name].start()

    def loaded(*wanted):
        for name in wanted:
            if name in loads:
                loads.pop(name).wait()

    barrier = pltpu.get_barrier_semaphore()
    friends = (*z_to.values(), *x_to.values(), *y_to.values(), y_far, twin, after, before)
    for friend in friends:
        pl.semaphore_signal(barrier, inc=1, device_id=friend, device_id_type=MESH)
    loaded("w_rows")
    pl.semaphore_wait(barrier, len(friends))

    moves = {}
    whole, x_cols, z_cols = pl.ds(0, CH), pl.ds(0, CUT), pl.ds(CUT, CH - CUT)
    every, rest = pl.ds(0, NY), pl.ds(1, NY - 1)
    half_z = {"u": pl.ds(0, 2), "d": pl.ds(2, 2)}

    def half_x(dz, way):
        groups = UP - 1 if dz in LESS_UP else UP
        return pl.ds(0, groups) if way == "u" else pl.ds(groups, NY - groups)

    own, near, far = pl.ds(0, 1), pl.ds(1, 2), pl.ds(3, 1)

    for k, device in ((1, y_to["u"]), (2, y_far), (3, y_to["d"])):
        moves[f"s{k}"] = (
            w_rows.at[:, owned(ymod(y + k))], wbuf.at[0, c, 0, NY - k], device, ()
        )
    moves["rim"] = (streams.at[:, pl.ds(TOK - ROWS, ROWS), :], sx.at[:, pl.ds(0, ROWS), :], after, ())
    moves["rimp"] = (prod.at[pl.ds(TOK, FILT), :], prod.at[pl.ds(0, FILT), :], after, ("sh1",))

    def along_z(name, step, way, slots, groups, cols, needs):
        src = (1 - step) % NZ if way == "u" else step - 1
        dst = (src - 1) % NZ if way == "u" else src + 1
        moves[name] = (
            wbuf.at[src, c, slots, groups, :, cols],
            wbuf.at[dst, c, slots, groups, :, cols],
            z_to[way],
            needs,
        )

    def along_x(name, dz, way, src, dst, groups, cols, needs):
        moves[name] = (
            wbuf.at[dz, c, src, groups, :, cols], wbuf.at[dz, c, dst, groups, :, cols], x_to[way], needs
        )

    spread = ("s1", "s2", "s3")
    begun = ("x0u", "x0d", "ex0u", "ex0d")
    from_z = {0: begun, 4: ("m4u", "m4d")}
    for way in "ud":
        near_slot = 2 if way == "u" else 1
        mine = w_rows.at[:, owned(y)]
        moves["em1" + way] = (mine, wbuf.at[7 if way == "u" else 1, c, 0, 0], z_to[way], ())
        along_z("m1" + way, 1, way, own, rest, whole, spread)
        moves["ex0" + way] = (mine, wbuf.at[0, c, near_slot, 0], x_to[way], ())
        along_x("x0" + way, 0, way, 0, near_slot, rest, whole, spread)
        for step in range(2, NZ // 2 + 1):
            last = step == NZ // 2
            groups = half_z[way] if last else every
            needs = ("m1" + way, "em1" + way) if step == 2 else (f"m{step - 1}{way}",)
            along_z(f"m{step}{way}", step, way, own, groups, whole, needs)
            along_z(f"n{step}{way}", step, way, near, groups, z_cols, (f"n{step - 1}{way}",))
            along_z(f"f{step}{way}", step, way, far, groups, z_cols, (f"f{step - 1}{way}",))
        along_z("n1" + way, 1, way, near, every, z_cols, begun)
        along_z("f1" + way, 1, way, far, every, z_cols, ("xx0u", "xx0d"))
        for dz in range(NZ):
            if dz not in from_z:
                step = min(dz, NZ - dz)
                ways = "d" if dz < NZ // 2 else "u"
                from_z[dz] = tuple(f"{kind}{step}{ways}" for kind in ("m", "em")[: 2 if step == 1 else 1])
            cols = x_cols if dz else whole
            if dz:
                along_x(f"x{dz}{way}", dz, way, 0, near_slot, every, cols, from_z[dz])
            needs = (f"x{dz}{way}",) if dz else ("x0" + way, "ex0" + way)
            along_x(f"xx{dz}{way}", dz, way, near_slot, 3, half_x(dz, way), cols, needs)
        for b in range(CH // BLK):
            per = BLK // 128
            chunk = pl.ds(b * per, per)
            half = pl.ds(b * per + (0 if way == "u" else per // 2), per // 2)
            group = 3 if way == "u" else 1
            moves[f"g{b}{way}"] = (gbuf.at[0, chunk], gbuf.at[group, chunk], y_to[way], (f"c{b}",))
            moves[f"h{b}{way}"] = (gbuf.at[group, half], gbuf.at[2, half], y_to[way], (f"g{b}{way}",))
    for dz in range(NZ):
        by_x = from_z[dz] + tuple(f"{kind}{dz}{way}" for kind in ("x", "xx") for way in "ud")
        step = min(dz, NZ - dz)
        ways = "ud" if dz == NZ // 2 else "d" if dz < NZ // 2 else "u"
        by_z = tuple(f"{kind}{step}{way}" for kind in ("n", "f") for way in ways) if dz else ()
        if dz == 0:
            by_x = ("own",) + spread + by_x
        if dz == NZ // 2:
            for name, cols, needs in (("t4x", x_cols, by_x), ("t4z", z_cols, by_z + from_z[dz])):
                part = wbuf.at[dz, c, :, :, :, cols]
                moves[name] = (part, part, twin, needs)
        else:
            moves[f"t{dz}"] = (wbuf.at[dz, c], wbuf.at[dz, c], twin, by_x + by_z)

    def short_rows(start, rows):
        def lane_block(b, carry):
            lanes = pl.ds(pl.multiple_of(b * 128, 128), 128)
            done = []
            for s in range(3):
                window = sx[s, pl.ds(start, rows + ROWS), lanes].astype(jnp.float32)
                total = None
                for j in range(SHORT):
                    term = taps[s, j : j + 1, lanes] * window[ROWS - j : ROWS - j + rows]
                    total = term if total is None else total + term
                done.append(total)
            query[pl.ds(start, rows), lanes] = done[0]
            prod[pl.ds(FILT + start, rows), lanes] = (done[1] * done[2]).astype(jnp.bfloat16)
            return carry

        lax.fori_loop(0, CH // 128, lane_block, 0)

    def short_last():
        loaded("streams", "short")
        short_rows(FILT, FILT)

    def short_first():
        short_rows(ROWS, FILT - ROWS)

    def short_edge():
        @pl.when(me == 0)
        def _():
            sx[:, 0:ROWS, :] = jnp.zeros((3, ROWS, CH), jnp.bfloat16)

        short_rows(0, ROWS)

    def filter_spectrum():
        loaded("medium", "fwd_a")

        for b in range(CH // BLK):
            lanes = pl.ds(b * BLK, BLK)
            spec[:, lanes] = jnp.dot(
                fwd_av[:, 0:FILT], med[:, lanes], preferred_element_type=jnp.float32
            )

    def own_spectrum(b):
        loaded("fwd_b")
        lanes = pl.ds(b * BLK, BLK)
        freq[:, lanes] = jnp.dot(
            fwd_bv[...], prod[EDGE:WIN, lanes], preferred_element_type=jnp.float32
        )

    edge_ready = []

    def conv_block(b):
        loaded("skip", "inv")
        if not edge_ready:
            edge_ready.append(b)

            @pl.when(me == 0)
            def _():
                prod[0:FILT, :] = jnp.zeros((FILT, CH), jnp.bfloat16)

        lanes = pl.ds(b * BLK, BLK)
        total = freq[:, lanes] + jnp.dot(
            fwd_av[...], prod[0:EDGE, lanes], preferred_element_type=jnp.float32
        )
        fr, fi = total[:HALF], total[HALF:]
        hr, hi = spec[0:HALF, lanes], spec[HALF:WIN, lanes]
        both = jnp.concatenate([fr * hr - fi * hi, fr * hi + fi * hr], axis=0).astype(jnp.bfloat16)
        mixed = jnp.dot(inv_v[...], both, preferred_element_type=jnp.float32)
        direct = gain[0:1, lanes] * prod[pl.ds(FILT, TOK), lanes].astype(jnp.float32)
        gated = (query[:, lanes] * (mixed + direct)).astype(jnp.bfloat16)
        for part in range(BLK // 128):
            gbuf[0, b * (BLK // 128) + part] = gated[:, part * 128 : (part + 1) * 128]

    stores = []

    def project(dz, blocks):
        loaded("residual")
        begin, end = dz == 0, dz == NZ // 2
        plane = lax.rem(z + dz, NZ)
        left = jnp.concatenate([gbuf[g, plane] for g in range(NY)], axis=1)
        for n in blocks:
            cols = pl.ds(n * BLK, BLK)
            pieces = []
            for g in range(NY):
                for xx in range(NX):
                    dx = lax.rem(xx - x + NX, NX)
                    slot = dx + dx // 2 - 2 * (dx // 3)
                    pieces += [wbuf[dz, cc, slot, g, :, cols] for cc in range(NC)]
            right = jnp.concatenate(pieces, axis=0)
            total = res[:, cols].astype(jnp.float32) if begin else acc[:, cols]
            total = total + jnp.dot(left, right, preferred_element_type=jnp.float32)
            if end:
                out[:, cols] = total.astype(jnp.bfloat16)
                store = pltpu.make_async_copy(out.at[:, cols], result.at[:, cols], local.at[N_LOADS + n])
                store.start()
                stores.append(store)
            else:
                acc[:, cols] = total

    tasks = {
        "sh1": (short_last, ()),
        "sh0": (short_first, ()),
        "spec": (filter_spectrum, ()),
        "fix": (short_edge, ("rim", "sh1")),
    }
    for b in range(CH // BLK):
        tasks[f"o{b}"] = (functools.partial(own_spectrum, b), ("sh1", "sh0"))
        tasks[f"c{b}"] = (functools.partial(conv_block, b), ("rimp", "fix", "spec", f"o{b}"))
    gated_all = tuple(f"{kind}{b}{way}" for kind in "gh" for b in range(CH // BLK) for way in "ud")
    count = CH // BLK
    others = tuple(f"p{dz}" for dz in range(NZ) if dz != NZ // 2)
    for dz in range(NZ):
        if dz == NZ // 2:
            early = CUT // BLK
            tasks["p4x"] = (functools.partial(project, dz, range(early)), ("t4x",) + others)
            tasks["p4"] = (functools.partial(project, dz, range(early, count)), ("t4x", "t4z") + others)
        else:
            needs = (f"t{dz}",) + (("p0",) if dz else gated_all)
            tasks[f"p{dz}"] = (functools.partial(project, dz, range(count)), needs)

    copies, seen, ran = {}, set(), set()

    def await_all(needs):
        for name in needs:
            if name == "own":
                loaded("w_out")
            elif name in tasks:
                assert name in ran
            elif name not in seen:
                seen.add(name)
                copies[name].wait_recv()

    assert sorted(ORDER) == sorted([*moves, *tasks])
    for name in ORDER:
        if name in tasks:
            task, needs = tasks[name]
            await_all(needs)
            task()
            ran.add(name)
            continue
        src, dst, device, needs = moves[name]
        await_all(needs)
        i = len(copies)
        copies[name] = pltpu.make_async_remote_copy(
            src_ref=src,
            dst_ref=dst,
            send_sem=send.at[i],
            recv_sem=recv.at[i],
            device_id=device,
            device_id_type=MESH,
        )
        copies[name].start()
    for store in stores:
        store.wait()
    await_all(copies)
    for copy in copies.values():
        copy.wait_send()


def on_device(streams, residual_in, short_filter, medium_filter, skip_gain, w_out):
    forward, inverse = transforms()
    fwd_a = jnp.asarray(forward[:, :EDGE].astype(np.float32), dtype=jnp.bfloat16)
    fwd_b = jnp.asarray(forward[:, EDGE:].astype(np.float32), dtype=jnp.bfloat16)
    inv = jnp.asarray(inverse.astype(np.float32), dtype=jnp.bfloat16)
    hbm = pl.BlockSpec(memory_space=pl.ANY)
    bf16, f32 = jnp.bfloat16, jnp.float32
    return pl.pallas_call(
        kernel,
        out_shape=jax.ShapeDtypeStruct((TOK, CH), bf16),
        in_specs=[hbm] * 9,
        out_specs=hbm,
        scratch_shapes=[
            pltpu.VMEM((3, ROWS + TOK, CH), bf16),
            pltpu.VMEM((3, SHORT, CH), f32),
            pltpu.VMEM((FILT, CH), bf16),
            pltpu.VMEM((1, CH), f32),
            pltpu.VMEM((WIN, EDGE), bf16),
            pltpu.VMEM((WIN, WIN - EDGE), bf16),
            pltpu.VMEM((TOK, WIN), bf16),
            pltpu.VMEM((TOK, CH), bf16),
            pltpu.VMEM((WIN, CH), bf16),
            pltpu.VMEM((TOK, CH), f32),
            pltpu.VMEM((WIN, CH), f32),
            pltpu.VMEM((WIN, CH), f32),
            pltpu.VMEM((NZ, NC, NX, NY, ROWS, CH), bf16),
            pltpu.VMEM((NY, CH // 128, TOK, 128), bf16),
            pltpu.VMEM((TOK, CH), f32),
            pltpu.VMEM((TOK, CH), bf16),
            pltpu.VMEM((ROWS, NY * CH), bf16),
            pltpu.SemaphoreType.DMA((N_COPIES,)),
            pltpu.SemaphoreType.DMA((N_COPIES,)),
            pltpu.SemaphoreType.DMA((N_LOADS + CH // BLK,)),
        ],
        compiler_params=pltpu.CompilerParams(
            collective_id=0, has_side_effects=True, vmem_limit_bytes=60 * 1024 * 1024
        ),
    )(streams, residual_in, short_filter, medium_filter, skip_gain.reshape(1, CH), w_out, fwd_a, fwd_b, inv)


def solution(mesh):
    placed = (
        P(None, "ctx", "ch"),
        P("ctx", "ch"),
        P(),
        P(None, "ch"),
        P("ch"),
        P(("ch", "ctx"), None),
    )
    return jax.shard_map(
        on_device, mesh=mesh, in_specs=placed, out_specs=P("ctx", "ch"), check_vma=False
    )
```

```python
import functools

import jax
import jax.numpy as jnp
import numpy as np
from jax import lax
from jax.experimental import pallas as pl
from jax.experimental.pallas import tpu as pltpu
from jax.sharding import PartitionSpec as P

MESH = pl.DeviceIdType.MESH
NZ, NX, NC, NY = 8, 4, 2, 4
TOK = 256
CH = 1024
FILT = 128
SHORT = 7
ROWS = 16
WIN = FILT + TOK
HALF = WIN // 2
BLK = 256
CUT = 640
UP = 2
LESS_UP = ()
EDGE = FILT + ROWS
N_COPIES = 128


def transforms():
    freq = np.arange(HALF) + 0.5
    angle = 2 * np.pi * np.outer(freq, np.arange(WIN)) / WIN
    forward = np.concatenate([np.cos(angle), -np.sin(angle)], axis=0)
    inverse = forward.T[FILT:] * (2.0 / WIN)
    return forward, inverse


ORDER = (
    "s2", "s1", "ex0u", "em1d", "s3", "em1u", "rim", "sh1", "rimp", "x0d", "m1u", "m1d", "ex0d", "spec", "sh0",
    "x0u", "fix", "o1", "o0", "x1d", "m2d", "x1u", "m2u", "xx0d", "o2", "c0", "xx0u", "x7u", "n1u", "x7d", "g0u",
    "n1d", "g0d", "c2", "x2d", "g2d", "xx1u", "m3d", "xx1d", "g2u", "x6u", "m3u", "x6d", "x2u", "c1", "f1d", "f1u",
    "xx7d", "o3", "c3", "g3d", "n2d", "g1u", "g3u", "n2u", "x3u", "t0", "h0u", "x5d", "m4d", "g1d", "m4u", "x3d",
    "xx7u", "f2u", "xx6d", "xx2d", "x5u", "f2d", "h2d", "n3d", "h0d", "xx6u", "n3u", "h2u", "x4u", "t7", "x4d",
    "f3d", "xx3u", "f3u", "xx2u", "xx3d", "h1u", "h3d", "n4d", "xx5d", "h3u", "xx5u", "h1d", "t6", "t1", "n4u",
    "xx4u", "xx4d", "f4d", "f4u", "t3", "t2", "t5", "p0", "t4x", "p7", "t4z", "p1", "p6", "p2", "p5", "p3", "p4x",
    "p4",
)
N_LOADS = 10


def kernel(
    streams, residual, short, medium, skip, w_out, fwd_a, fwd_b, inv,
    result,
    sx, taps, med, gain, fwd_av, fwd_bv, inv_v, res, prod, query, spec, freq, wbuf, gbuf, acc, out, w_rows,
    send, recv, local,
):
    me, y = lax.axis_index("ctx"), lax.axis_index("ch")
    c = lax.rem(me, NC)
    x = lax.rem(me // NC, NX)
    z = me // (NC * NX)

    def at(zz, xx, cc):
        return (lax.rem(zz + NZ, NZ) * NX + lax.rem(xx + NX, NX)) * NC + cc

    def ymod(v):
        return lax.rem(v + NY, NY)

    n_ctx = NZ * NX * NC
    z_to = {"u": (at(z + 1, x, c), y), "d": (at(z - 1, x, c), y)}
    x_to = {"u": (at(z, x + 1, c), y), "d": (at(z, x - 1, c), y)}
    y_to = {"u": (me, ymod(y + 1)), "d": (me, ymod(y - 1))}
    twin, y_far = (at(z, x, 1 - c), y), (me, ymod(y + 2))
    after, before = (lax.rem(me + 1, n_ctx), y), (lax.rem(me + n_ctx - 1, n_ctx), y)

    def owned(group):
        return pl.ds(pl.multiple_of(group * CH, CH), CH)

    loads = {}
    for i, (name, src, dst) in enumerate(
        (
            ("w_rows", w_out, w_rows),
            ("streams", streams, sx.at[:, pl.ds(ROWS, TOK), :]),
            ("short", short.at[:, :, owned(y)], taps),
            ("w_out", w_out.at[:, owned(y)], wbuf.at[0, c, 0, 0]),
            ("medium", medium, med),
            ("fwd_a", fwd_a, fwd_av),
            ("fwd_b", fwd_b, fwd_bv),
            ("skip", skip, gain),
            ("inv", inv, inv_v),
            ("residual", residual, res),
        )
    ):
        loads[name] = pltpu.make_async_copy(src, dst, local.at[i])
        loads[name].start()

    def loaded(*wanted):
        for name in wanted:
            if name in loads:
                loads.pop(name).wait()

    barrier = pltpu.get_barrier_semaphore()
    friends = (*z_to.values(), *x_to.values(), *y_to.values(), y_far, twin, after, before)
    for friend in friends:
        pl.semaphore_signal(barrier, inc=1, device_id=friend, device_id_type=MESH)
    loaded("w_rows")
    pl.semaphore_wait(barrier, len(friends))

    moves = {}
    whole, x_cols, z_cols = pl.ds(0, CH), pl.ds(0, CUT), pl.ds(CUT, CH - CUT)
    every, rest = pl.ds(0, NY), pl.ds(1, NY - 1)
    half_z = {"u": pl.ds(0, 2), "d": pl.ds(2, 2)}

    def half_x(dz, way):
        groups = UP - 1 if dz in LESS_UP else UP
        return pl.ds(0, groups) if way == "u" else pl.ds(groups, NY - groups)

    own, near, far = pl.ds(0, 1), pl.ds(1, 2), pl.ds(3, 1)

    for k, device in ((1, y_to["u"]), (2, y_far), (3, y_to["d"])):
        moves[f"s{k}"] = (
            w_rows.at[:, owned(ymod(y + k))], wbuf.at[0, c, 0, NY - k], device, ()
        )
    moves["rim"] = (streams.at[:, pl.ds(TOK - ROWS, ROWS), :], sx.at[:, pl.ds(0, ROWS), :], after, ())
    moves["rimp"] = (prod.at[pl.ds(TOK, FILT), :], prod.at[pl.ds(0, FILT), :], after, ("sh1",))

    def along_z(name, step, way, slots, groups, cols, needs):
        src = (1 - step) % NZ if way == "u" else step - 1
        dst = (src - 1) % NZ if way == "u" else src + 1
        moves[name] = (
            wbuf.at[src, c, slots, groups, :, cols],
            wbuf.at[dst, c, slots, groups, :, cols],
            z_to[way],
            needs,
        )

    def along_x(name, dz, way, src, dst, groups, cols, needs):
        moves[name] = (
            wbuf.at[dz, c, src, groups, :, cols], wbuf.at[dz, c, dst, groups, :, cols], x_to[way], needs
        )

    spread = ("s1", "s2", "s3")
    begun = ("x0u", "x0d", "ex0u", "ex0d")
    from_z = {0: begun, 4: ("m4u", "m4d")}
    for way in "ud":
        near_slot = 2 if way == "u" else 1
        mine = w_rows.at[:, owned(y)]
        moves["em1" + way] = (mine, wbuf.at[7 if way == "u" else 1, c, 0, 0], z_to[way], ())
        along_z("m1" + way, 1, way, own, rest, whole, spread)
        moves["ex0" + way] = (mine, wbuf.at[0, c, near_slot, 0], x_to[way], ())
        along_x("x0" + way, 0, way, 0, near_slot, rest, whole, spread)
        for step in range(2, NZ // 2 + 1):
            last = step == NZ // 2
            groups = half_z[way] if last else every
            needs = ("m1" + way, "em1" + way) if step == 2 else (f"m{step - 1}{way}",)
            along_z(f"m{step}{way}", step, way, own, groups, whole, needs)
            along_z(f"n{step}{way}", step, way, near, groups, z_cols, (f"n{step - 1}{way}",))
            along_z(f"f{step}{way}", step, way, far, groups, z_cols, (f"f{step - 1}{way}",))
        along_z("n1" + way, 1, way, near, every, z_cols, begun)
        along_z("f1" + way, 1, way, far, every, z_cols, ("xx0u", "xx0d"))
        for dz in range(NZ):
            if dz not in from_z:
                step = min(dz, NZ - dz)
                ways = "d" if dz < NZ // 2 else "u"
                from_z[dz] = tuple(f"{kind}{step}{ways}" for kind in ("m", "em")[: 2 if step == 1 else 1])
            cols = x_cols if dz else whole
            if dz:
                along_x(f"x{dz}{way}", dz, way, 0, near_slot, every, cols, from_z[dz])
            needs = (f"x{dz}{way}",) if dz else ("x0" + way, "ex0" + way)
            along_x(f"xx{dz}{way}", dz, way, near_slot, 3, half_x(dz, way), cols, needs)
        for b in range(CH // BLK):
            per = BLK // 128
            chunk = pl.ds(b * per, per)
            half = pl.ds(b * per + (0 if way == "u" else per // 2), per // 2)
            group = 3 if way == "u" else 1
            moves[f"g{b}{way}"] = (gbuf.at[0, chunk], gbuf.at[group, chunk], y_to[way], (f"c{b}",))
            moves[f"h{b}{way}"] = (gbuf.at[group, half], gbuf.at[2, half], y_to[way], (f"g{b}{way}",))
    for dz in range(NZ):
        by_x = from_z[dz] + tuple(f"{kind}{dz}{way}" for kind in ("x", "xx") for way in "ud")
        step = min(dz, NZ - dz)
        ways = "ud" if dz == NZ // 2 else "d" if dz < NZ // 2 else "u"
        by_z = tuple(f"{kind}{step}{way}" for kind in ("n", "f") for way in ways) if dz else ()
        if dz == 0:
            by_x = ("own",) + spread + by_x
        if dz == NZ // 2:
            for name, cols, needs in (("t4x", x_cols, by_x), ("t4z", z_cols, by_z + from_z[dz])):
                part = wbuf.at[dz, c, :, :, :, cols]
                moves[name] = (part, part, twin, needs)
        else:
            moves[f"t{dz}"] = (wbuf.at[dz, c], wbuf.at[dz, c], twin, by_x + by_z)

    def short_rows(start, rows):
        def lane_block(b, carry):
            lanes = pl.ds(pl.multiple_of(b * 128, 128), 128)
            done = []
            for s in range(3):
                window = sx[s, pl.ds(start, rows + ROWS), lanes].astype(jnp.float32)
                total = None
                for j in range(SHORT):
                    term = taps[s, j : j + 1, lanes] * window[ROWS - j : ROWS - j + rows]
                    total = term if total is None else total + term
                done.append(total)
            query[pl.ds(start, rows), lanes] = done[0]
            prod[pl.ds(FILT + start, rows), lanes] = (done[1] * done[2]).astype(jnp.bfloat16)
            return carry

        lax.fori_loop(0, CH // 128, lane_block, 0)

    def short_last():
        loaded("streams", "short")
        short_rows(FILT, FILT)

    def short_first():
        short_rows(ROWS, FILT - ROWS)

    def short_edge():
        @pl.when(me == 0)
        def _():
            sx[:, 0:ROWS, :] = jnp.zeros((3, ROWS, CH), jnp.bfloat16)

        short_rows(0, ROWS)

    def filter_spectrum():
        loaded("medium", "fwd_a")

        for b in range(CH // BLK):
            lanes = pl.ds(b * BLK, BLK)
            spec[:, lanes] = jnp.dot(
                fwd_av[:, 0:FILT], med[:, lanes], preferred_element_type=jnp.float32
            )

    def own_spectrum(b):
        loaded("fwd_b")
        lanes = pl.ds(b * BLK, BLK)
        freq[:, lanes] = jnp.dot(
            fwd_bv[...], prod[EDGE:WIN, lanes], preferred_element_type=jnp.float32
        )

    edge_ready = []

    def conv_block(b):
        loaded("skip", "inv")
        if not edge_ready:
            edge_ready.append(b)

            @pl.when(me == 0)
            def _():
                prod[0:FILT, :] = jnp.zeros((FILT, CH), jnp.bfloat16)

        lanes = pl.ds(b * BLK, BLK)
        total = freq[:, lanes] + jnp.dot(
            fwd_av[...], prod[0:EDGE, lanes], preferred_element_type=jnp.float32
        )
        fr, fi = total[:HALF], total[HALF:]
        hr, hi = spec[0:HALF, lanes], spec[HALF:WIN, lanes]
        both = jnp.concatenate([fr * hr - fi * hi, fr * hi + fi * hr], axis=0).astype(jnp.bfloat16)
        mixed = jnp.dot(inv_v[...], both, preferred_element_type=jnp.float32)
        direct = gain[0:1, lanes] * prod[pl.ds(FILT, TOK), lanes].astype(jnp.float32)
        gated = (query[:, lanes] * (mixed + direct)).astype(jnp.bfloat16)
        for part in range(BLK // 128):
            gbuf[0, b * (BLK // 128) + part] = gated[:, part * 128 : (part + 1) * 128]

    stores = []

    def project(dz, blocks):
        loaded("residual")
        begin, end = dz == 0, dz == NZ // 2
        plane = lax.rem(z + dz, NZ)
        left = jnp.concatenate([gbuf[g, plane] for g in range(NY)], axis=1)
        for n in blocks:
            cols = pl.ds(n * BLK, BLK)
            pieces = []
            for g in range(NY):
                for xx in range(NX):
                    dx = lax.rem(xx - x + NX, NX)
                    slot = dx + dx // 2 - 2 * (dx // 3)
                    pieces += [wbuf[dz, cc, slot, g, :, cols] for cc in range(NC)]
            right = jnp.concatenate(pieces, axis=0)
            total = res[:, cols].astype(jnp.float32) if begin else acc[:, cols]
            total = total + jnp.dot(left, right, preferred_element_type=jnp.float32)
            if end:
                out[:, cols] = total.astype(jnp.bfloat16)
                store = pltpu.make_async_copy(out.at[:, cols], result.at[:, cols], local.at[N_LOADS + n])
                store.start()
                stores.append(store)
            else:
                acc[:, cols] = total

    tasks = {
        "sh1": (short_last, ()),
        "sh0": (short_first, ()),
        "spec": (filter_spectrum, ()),
        "fix": (short_edge, ("rim", "sh1")),
    }
    for b in range(CH // BLK):
        tasks[f"o{b}"] = (functools.partial(own_spectrum, b), ("sh1", "sh0"))
        tasks[f"c{b}"] = (functools.partial(conv_block, b), ("rimp", "fix", "spec", f"o{b}"))
    gated_all = tuple(f"{kind}{b}{way}" for kind in "gh" for b in range(CH // BLK) for way in "ud")
    count = CH // BLK
    others = tuple(f"p{dz}" for dz in range(NZ) if dz != NZ // 2)
    for dz in range(NZ):
        if dz == NZ // 2:
            early = CUT // BLK
            tasks["p4x"] = (functools.partial(project, dz, range(early)), ("t4x",) + others)
            tasks["p4"] = (functools.partial(project, dz, range(early, count)), ("t4x", "t4z") + others)
        else:
            needs = (f"t{dz}",) + (("p0",) if dz else gated_all)
            tasks[f"p{dz}"] = (functools.partial(project, dz, range(count)), needs)

    copies, seen, ran = {}, set(), set()

    def await_all(needs):
        for name in needs:
            if name == "own":
                loaded("w_out")
            elif name in tasks:
                assert name in ran
            elif name not in seen:
                seen.add(name)
                copies[name].wait_recv()

    assert sorted(ORDER) == sorted([*moves, *tasks])
    for name in ORDER:
        if name in tasks:
            task, needs = tasks[name]
            await_all(needs)
            task()
            ran.add(name)
            continue
        src, dst, device, needs = moves[name]
        await_all(needs)
        i = len(copies)
        copies[name] = pltpu.make_async_remote_copy(
            src_ref=src,
            dst_ref=dst,
            send_sem=send.at[i],
            recv_sem=recv.at[i],
            device_id=device,
            device_id_type=MESH,
        )
        copies[name].start()
    for store in stores:
        store.wait()
    await_all(copies)
    for copy in copies.values():
        copy.wait_send()


def on_device(streams, residual_in, short_filter, medium_filter, skip_gain, w_out):
    forward, inverse = transforms()
    fwd_a = jnp.asarray(forward[:, :EDGE].astype(np.float32), dtype=jnp.bfloat16)
    fwd_b = jnp.asarray(forward[:, EDGE:].astype(np.float32), dtype=jnp.bfloat16)
    inv = jnp.asarray(inverse.astype(np.float32), dtype=jnp.bfloat16)
    hbm = pl.BlockSpec(memory_space=pl.ANY)
    bf16, f32 = jnp.bfloat16, jnp.float32
    return pl.pallas_call(
        kernel,
        out_shape=jax.ShapeDtypeStruct((TOK, CH), bf16),
        in_specs=[hbm] * 9,
        out_specs=hbm,
        scratch_shapes=[
            pltpu.VMEM((3, ROWS + TOK, CH), bf16),
            pltpu.VMEM((3, SHORT, CH), f32),
            pltpu.VMEM((FILT, CH), bf16),
            pltpu.VMEM((1, CH), f32),
            pltpu.VMEM((WIN, EDGE), bf16),
            pltpu.VMEM((WIN, WIN - EDGE), bf16),
            pltpu.VMEM((TOK, WIN), bf16),
            pltpu.VMEM((TOK, CH), bf16),
            pltpu.VMEM((WIN, CH), bf16),
            pltpu.VMEM((TOK, CH), f32),
            pltpu.VMEM((WIN, CH), f32),
            pltpu.VMEM((WIN, CH), f32),
            pltpu.VMEM((NZ, NC, NX, NY, ROWS, CH), bf16),
            pltpu.VMEM((NY, CH // 128, TOK, 128), bf16),
            pltpu.VMEM((TOK, CH), f32),
            pltpu.VMEM((TOK, CH), bf16),
            pltpu.VMEM((ROWS, NY * CH), bf16),
            pltpu.SemaphoreType.DMA((N_COPIES,)),
            pltpu.SemaphoreType.DMA((N_COPIES,)),
            pltpu.SemaphoreType.DMA((N_LOADS + CH // BLK,)),
        ],
        compiler_params=pltpu.CompilerParams(
            collective_id=0, has_side_effects=True, vmem_limit_bytes=60 * 1024 * 1024
        ),
    )(streams, residual_in, short_filter, medium_filter, skip_gain.reshape(1, CH), w_out, fwd_a, fwd_b, inv)


def solution(mesh):
    placed = (
        P(None, "ctx", "ch"),
        P("ctx", "ch"),
        P(),
        P(None, "ch"),
        P("ch"),
        P(("ch", "ctx"), None),
    )
    return jax.shard_map(
        on_device, mesh=mesh, in_specs=placed, out_specs=P("ctx", "ch"), check_vma=False
    )
```

```python
import functools

import jax
import jax.numpy as jnp
import numpy as np
from jax import lax
from jax.experimental import pallas as pl
from jax.experimental.pallas import tpu as pltpu
from jax.sharding import PartitionSpec as P

MESH = pl.DeviceIdType.MESH
NZ, NX, NC, NY = 8, 4, 2, 4
TOK = 256
CH = 1024
FILT = 128
SHORT = 7
ROWS = 16
WIN = FILT + TOK
HALF = WIN // 2
BLK = 256
CUT = 640
UP = 2
LESS_UP = ()
EDGE = FILT + ROWS
N_COPIES = 128


def transforms():
    freq = np.arange(HALF) + 0.5
    angle = 2 * np.pi * np.outer(freq, np.arange(WIN)) / WIN
    forward = np.concatenate([np.cos(angle), -np.sin(angle)], axis=0)
    inverse = forward.T[FILT:] * (2.0 / WIN)
    return forward, inverse


ORDER = (
    "s2", "s1", "ex0u", "em1d", "s3", "em1u", "rim", "sh1", "rimp", "x0d", "m1u", "m1d", "ex0d", "spec", "sh0",
    "x0u", "fix", "o1", "o0", "x1d", "m2d", "x1u", "m2u", "xx0d", "o2", "c0", "xx0u", "x7u", "n1u", "x7d", "g0u",
    "n1d", "g0d", "c2", "x2d", "g2d", "xx1u", "m3d", "xx1d", "g2u", "x6u", "m3u", "x6d", "x2u", "c1", "f1d", "f1u",
    "xx7d", "o3", "c3", "g3d", "n2d", "g1u", "g3u", "n2u", "x3u", "t0", "h0u", "x5d", "m4d", "g1d", "m4u", "x3d",
    "xx7u", "f2u", "xx6d", "xx2d", "x5u", "f2d", "h2d", "n3d", "h0d", "xx6u", "n3u", "h2u", "x4u", "t7", "x4d",
    "f3d", "xx3u", "f3u", "xx2u", "xx3d", "h1u", "h3d", "n4d", "xx5d", "h3u", "xx5u", "h1d", "t6", "t1", "n4u",
    "xx4u", "xx4d", "f4d", "f4u", "t3", "t2", "t5", "p0", "t4x", "p7", "t4z", "p1", "p6", "p2", "p5", "p3", "p4x",
    "p4",
)
N_LOADS = 10


def kernel(
    streams, residual, short, medium, skip, w_out, fwd_a, fwd_b, inv,
    result,
    sx, taps, med, gain, fwd_av, fwd_bv, inv_v, res, prod, query, spec, freq, wbuf, gbuf, acc, out, w_rows,
    send, recv, local,
):
    me, y = lax.axis_index("ctx"), lax.axis_index("ch")
    c = lax.rem(me, NC)
    x = lax.rem(me // NC, NX)
    z = me // (NC * NX)

    def at(zz, xx, cc):
        return (lax.rem(zz + NZ, NZ) * NX + lax.rem(xx + NX, NX)) * NC + cc

    def ymod(v):
        return lax.rem(v + NY, NY)

    n_ctx = NZ * NX * NC
    z_to = {"u": (at(z + 1, x, c), y), "d": (at(z - 1, x, c), y)}
    x_to = {"u": (at(z, x + 1, c), y), "d": (at(z, x - 1, c), y)}
    y_to = {"u": (me, ymod(y + 1)), "d": (me, ymod(y - 1))}
    twin, y_far = (at(z, x, 1 - c), y), (me, ymod(y + 2))
    after, before = (lax.rem(me + 1, n_ctx), y), (lax.rem(me + n_ctx - 1, n_ctx), y)

    def owned(group):
        return pl.ds(pl.multiple_of(group * CH, CH), CH)

    loads = {}
    for i, (name, src, dst) in enumerate(
        (
            ("w_rows", w_out, w_rows),
            ("streams", streams, sx.at[:, pl.ds(ROWS, TOK), :]),
            ("short", short.at[:, :, owned(y)], taps),
            ("w_out", w_out.at[:, owned(y)], wbuf.at[0, c, 0, 0]),
            ("medium", medium, med),
            ("fwd_a", fwd_a, fwd_av),
            ("fwd_b", fwd_b, fwd_bv),
            ("skip", skip, gain),
            ("inv", inv, inv_v),
            ("residual", residual, res),
        )
    ):
        loads[name] = pltpu.make_async_copy(src, dst, local.at[i])
        loads[name].start()

    def loaded(*wanted):
        for name in wanted:
            if name in loads:
                loads.pop(name).wait()

    barrier = pltpu.get_barrier_semaphore()
    friends = (*z_to.values(), *x_to.values(), *y_to.values(), y_far, twin, after, before)
    for friend in friends:
        pl.semaphore_signal(barrier, inc=1, device_id=friend, device_id_type=MESH)
    loaded("w_rows")
    pl.semaphore_wait(barrier, len(friends))

    moves = {}
    whole, x_cols, z_cols = pl.ds(0, CH), pl.ds(0, CUT), pl.ds(CUT, CH - CUT)
    every, rest = pl.ds(0, NY), pl.ds(1, NY - 1)
    half_z = {"u": pl.ds(0, 2), "d": pl.ds(2, 2)}

    def half_x(dz, way):
        groups = UP - 1 if dz in LESS_UP else UP
        return pl.ds(0, groups) if way == "u" else pl.ds(groups, NY - groups)

    own, near, far = pl.ds(0, 1), pl.ds(1, 2), pl.ds(3, 1)

    for k, device in ((1, y_to["u"]), (2, y_far), (3, y_to["d"])):
        moves[f"s{k}"] = (
            w_rows.at[:, owned(ymod(y + k))], wbuf.at[0, c, 0, NY - k], device, ()
        )
    moves["rim"] = (streams.at[:, pl.ds(TOK - ROWS, ROWS), :], sx.at[:, pl.ds(0, ROWS), :], after, ())
    moves["rimp"] = (prod.at[pl.ds(TOK, FILT), :], prod.at[pl.ds(0, FILT), :], after, ("sh1",))

    def along_z(name, step, way, slots, groups, cols, needs):
        src = (1 - step) % NZ if way == "u" else step - 1
        dst = (src - 1) % NZ if way == "u" else src + 1
        moves[name] = (
            wbuf.at[src, c, slots, groups, :, cols],
            wbuf.at[dst, c, slots, groups, :, cols],
            z_to[way],
            needs,
        )

    def along_x(name, dz, way, src, dst, groups, cols, needs):
        moves[name] = (
            wbuf.at[dz, c, src, groups, :, cols], wbuf.at[dz, c, dst, groups, :, cols], x_to[way], needs
        )

    spread = ("s1", "s2", "s3")
    begun = ("x0u", "x0d", "ex0u", "ex0d")
    from_z = {0: begun, 4: ("m4u", "m4d")}
    for way in "ud":
        near_slot = 2 if way == "u" else 1
        mine = w_rows.at[:, owned(y)]
        moves["em1" + way] = (mine, wbuf.at[7 if way == "u" else 1, c, 0, 0], z_to[way], ())
        along_z("m1" + way, 1, way, own, rest, whole, spread)
        moves["ex0" + way] = (mine, wbuf.at[0, c, near_slot, 0], x_to[way], ())
        along_x("x0" + way, 0, way, 0, near_slot, rest, whole, spread)
        for step in range(2, NZ // 2 + 1):
            last = step == NZ // 2
            groups = half_z[way] if last else every
            needs = ("m1" + way, "em1" + way) if step == 2 else (f"m{step - 1}{way}",)
            along_z(f"m{step}{way}", step, way, own, groups, whole, needs)
            along_z(f"n{step}{way}", step, way, near, groups, z_cols, (f"n{step - 1}{way}",))
            along_z(f"f{step}{way}", step, way, far, groups, z_cols, (f"f{step - 1}{way}",))
        along_z("n1" + way, 1, way, near, every, z_cols, begun)
        along_z("f1" + way, 1, way, far, every, z_cols, ("xx0u", "xx0d"))
        for dz in range(NZ):
            if dz not in from_z:
                step = min(dz, NZ - dz)
                ways = "d" if dz < NZ // 2 else "u"
                from_z[dz] = tuple(f"{kind}{step}{ways}" for kind in ("m", "em")[: 2 if step == 1 else 1])
            cols = x_cols if dz else whole
            if dz:
                along_x(f"x{dz}{way}", dz, way, 0, near_slot, every, cols, from_z[dz])
            needs = (f"x{dz}{way}",) if dz else ("x0" + way, "ex0" + way)
            along_x(f"xx{dz}{way}", dz, way, near_slot, 3, half_x(dz, way), cols, needs)
        for b in range(CH // BLK):
            per = BLK // 128
            chunk = pl.ds(b * per, per)
            half = pl.ds(b * per + (0 if way == "u" else per // 2), per // 2)
            group = 3 if way == "u" else 1
            moves[f"g{b}{way}"] = (gbuf.at[0, chunk], gbuf.at[group, chunk], y_to[way], (f"c{b}",))
            moves[f"h{b}{way}"] = (gbuf.at[group, half], gbuf.at[2, half], y_to[way], (f"g{b}{way}",))
    for dz in range(NZ):
        by_x = from_z[dz] + tuple(f"{kind}{dz}{way}" for kind in ("x", "xx") for way in "ud")
        step = min(dz, NZ - dz)
        ways = "ud" if dz == NZ // 2 else "d" if dz < NZ // 2 else "u"
        by_z = tuple(f"{kind}{step}{way}" for kind in ("n", "f") for way in ways) if dz else ()
        if dz == 0:
            by_x = ("own",) + spread + by_x
        if dz == NZ // 2:
            for name, cols, needs in (("t4x", x_cols, by_x), ("t4z", z_cols, by_z + from_z[dz])):
                part = wbuf.at[dz, c, :, :, :, cols]
                moves[name] = (part, part, twin, needs)
        else:
            moves[f"t{dz}"] = (wbuf.at[dz, c], wbuf.at[dz, c], twin, by_x + by_z)

    def short_rows(start, rows):
        def lane_block(b, carry):
            lanes = pl.ds(pl.multiple_of(b * BLK, BLK), BLK)
            done = []
            for s in range(3):
                window = sx[s, pl.ds(start, rows + ROWS), lanes].astype(jnp.float32)
                total = None
                for j in range(SHORT):
                    term = taps[s, j : j + 1, lanes] * window[ROWS - j : ROWS - j + rows]
                    total = term if total is None else total + term
                done.append(total)
            query[pl.ds(start, rows), lanes] = done[0]
            prod[pl.ds(FILT + start, rows), lanes] = (done[1] * done[2]).astype(jnp.bfloat16)
            return carry

        lax.fori_loop(0, CH // BLK, lane_block, 0)

    def short_last():
        loaded("streams", "short")
        short_rows(FILT, FILT)

    def short_first():
        short_rows(ROWS, FILT - ROWS)

    def short_edge():
        @pl.when(me == 0)
        def _():
            sx[:, 0:ROWS, :] = jnp.zeros((3, ROWS, CH), jnp.bfloat16)

        short_rows(0, ROWS)

    def filter_spectrum():
        loaded("medium", "fwd_a")

        for b in range(CH // BLK):
            lanes = pl.ds(b * BLK, BLK)
            spec[:, lanes] = jnp.dot(
                fwd_av[:, 0:FILT], med[:, lanes], preferred_element_type=jnp.float32
            )

    def own_spectrum(b):
        loaded("fwd_b")
        lanes = pl.ds(b * BLK, BLK)
        freq[:, lanes] = jnp.dot(
            fwd_bv[...], prod[EDGE:WIN, lanes], preferred_element_type=jnp.float32
        )

    edge_ready = []

    def conv_block(b):
        loaded("skip", "inv")
        if not edge_ready:
            edge_ready.append(b)

            @pl.when(me == 0)
            def _():
                prod[0:FILT, :] = jnp.zeros((FILT, CH), jnp.bfloat16)

        lanes = pl.ds(b * BLK, BLK)
        total = freq[:, lanes] + jnp.dot(
            fwd_av[...], prod[0:EDGE, lanes], preferred_element_type=jnp.float32
        )
        fr, fi = total[:HALF], total[HALF:]
        hr, hi = spec[0:HALF, lanes], spec[HALF:WIN, lanes]
        both = jnp.concatenate([fr * hr - fi * hi, fr * hi + fi * hr], axis=0).astype(jnp.bfloat16)
        mixed = jnp.dot(inv_v[...], both, preferred_element_type=jnp.float32)
        direct = gain[0:1, lanes] * prod[pl.ds(FILT, TOK), lanes].astype(jnp.float32)
        gated = (query[:, lanes] * (mixed + direct)).astype(jnp.bfloat16)
        for part in range(BLK // 128):
            gbuf[0, b * (BLK // 128) + part] = gated[:, part * 128 : (part + 1) * 128]

    stores = []

    def project(dz, blocks):
        loaded("residual")
        begin, end = dz == 0, dz == NZ // 2
        plane = lax.rem(z + dz, NZ)
        left = jnp.concatenate([gbuf[g, plane] for g in range(NY)], axis=1)
        for n in blocks:
            cols = pl.ds(n * BLK, BLK)
            pieces = []
            for g in range(NY):
                for xx in range(NX):
                    dx = lax.rem(xx - x + NX, NX)
                    slot = dx + dx // 2 - 2 * (dx // 3)
                    pieces += [wbuf[dz, cc, slot, g, :, cols] for cc in range(NC)]
            right = jnp.concatenate(pieces, axis=0)
            total = res[:, cols].astype(jnp.float32) if begin else acc[:, cols]
            total = total + jnp.dot(left, right, preferred_element_type=jnp.float32)
            if end:
                out[:, cols] = total.astype(jnp.bfloat16)
                store = pltpu.make_async_copy(out.at[:, cols], result.at[:, cols], local.at[N_LOADS + n])
                store.start()
                stores.append(store)
            else:
                acc[:, cols] = total

    tasks = {
        "sh1": (short_last, ()),
        "sh0": (short_first, ()),
        "spec": (filter_spectrum, ()),
        "fix": (short_edge, ("rim", "sh1")),
    }
    for b in range(CH // BLK):
        tasks[f"o{b}"] = (functools.partial(own_spectrum, b), ("sh1", "sh0"))
        tasks[f"c{b}"] = (functools.partial(conv_block, b), ("rimp", "fix", "spec", f"o{b}"))
    gated_all = tuple(f"{kind}{b}{way}" for kind in "gh" for b in range(CH // BLK) for way in "ud")
    count = CH // BLK
    others = tuple(f"p{dz}" for dz in range(NZ) if dz != NZ // 2)
    for dz in range(NZ):
        if dz == NZ // 2:
            early = CUT // BLK
            tasks["p4x"] = (functools.partial(project, dz, range(early)), ("t4x",) + others)
            tasks["p4"] = (functools.partial(project, dz, range(early, count)), ("t4x", "t4z") + others)
        else:
            needs = (f"t{dz}",) + (("p0",) if dz else gated_all)
            tasks[f"p{dz}"] = (functools.partial(project, dz, range(count)), needs)

    copies, seen, ran = {}, set(), set()

    def await_all(needs):
        for name in needs:
            if name == "own":
                loaded("w_out")
            elif name in tasks:
                assert name in ran
            elif name not in seen:
                seen.add(name)
                copies[name].wait_recv()

    assert sorted(ORDER) == sorted([*moves, *tasks])
    for name in ORDER:
        if name in tasks:
            task, needs = tasks[name]
            await_all(needs)
            task()
            ran.add(name)
            continue
        src, dst, device, needs = moves[name]
        await_all(needs)
        i = len(copies)
        copies[name] = pltpu.make_async_remote_copy(
            src_ref=src,
            dst_ref=dst,
            send_sem=send.at[i],
            recv_sem=recv.at[i],
            device_id=device,
            device_id_type=MESH,
        )
        copies[name].start()
    for store in stores:
        store.wait()
    await_all(copies)
    for copy in copies.values():
        copy.wait_send()


def on_device(streams, residual_in, short_filter, medium_filter, skip_gain, w_out):
    forward, inverse = transforms()
    fwd_a = jnp.asarray(forward[:, :EDGE].astype(np.float32), dtype=jnp.bfloat16)
    fwd_b = jnp.asarray(forward[:, EDGE:].astype(np.float32), dtype=jnp.bfloat16)
    inv = jnp.asarray(inverse.astype(np.float32), dtype=jnp.bfloat16)
    hbm = pl.BlockSpec(memory_space=pl.ANY)
    bf16, f32 = jnp.bfloat16, jnp.float32
    return pl.pallas_call(
        kernel,
        out_shape=jax.ShapeDtypeStruct((TOK, CH), bf16),
        in_specs=[hbm] * 9,
        out_specs=hbm,
        scratch_shapes=[
            pltpu.VMEM((3, ROWS + TOK, CH), bf16),
            pltpu.VMEM((3, SHORT, CH), f32),
            pltpu.VMEM((FILT, CH), bf16),
            pltpu.VMEM((1, CH), f32),
            pltpu.VMEM((WIN, EDGE), bf16),
            pltpu.VMEM((WIN, WIN - EDGE), bf16),
            pltpu.VMEM((TOK, WIN), bf16),
            pltpu.VMEM((TOK, CH), bf16),
            pltpu.VMEM((WIN, CH), bf16),
            pltpu.VMEM((TOK, CH), f32),
            pltpu.VMEM((WIN, CH), f32),
            pltpu.VMEM((WIN, CH), f32),
            pltpu.VMEM((NZ, NC, NX, NY, ROWS, CH), bf16),
            pltpu.VMEM((NY, CH // 128, TOK, 128), bf16),
            pltpu.VMEM((TOK, CH), f32),
            pltpu.VMEM((TOK, CH), bf16),
            pltpu.VMEM((ROWS, NY * CH), bf16),
            pltpu.SemaphoreType.DMA((N_COPIES,)),
            pltpu.SemaphoreType.DMA((N_COPIES,)),
            pltpu.SemaphoreType.DMA((N_LOADS + CH // BLK,)),
        ],
        compiler_params=pltpu.CompilerParams(
            collective_id=0, has_side_effects=True, vmem_limit_bytes=60 * 1024 * 1024
        ),
    )(streams, residual_in, short_filter, medium_filter, skip_gain.reshape(1, CH), w_out, fwd_a, fwd_b, inv)


def solution(mesh):
    placed = (
        P(None, "ctx", "ch"),
        P("ctx", "ch"),
        P(),
        P(None, "ch"),
        P("ch"),
        P(("ch", "ctx"), None),
    )
    return jax.shard_map(
        on_device, mesh=mesh, in_specs=placed, out_specs=P("ctx", "ch"), check_vma=False
    )
```
